128 devices in a mesh: ctx: 16 (over z_lo, y, core), head: 8 (over x, z_hi).
Axes of the slice: x: 4, y: 4, z: 4 (z_hi: 2, z_lo: 2; z = z_hi * 2 + z_lo), core: 2. Of those that a mesh axis runs over, the one named last changes fastest.
Arguments:
- main_queries: bfloat16 [4096, 128, 576], P('ctx', 'head'), may hold values from -6 to 6
- latents: bfloat16 [4096, 576], P('ctx'), may hold values from -6 to 6
- saved_lse: float32 [4096, 128], P('ctx', 'head'), may hold values from 9 to 12
- index_queries: bfloat16 [4096, 64, 128], P('ctx', 'head'), may hold values from -7 to 7, as said below
- index_keys: bfloat16 [4096, 128], P('ctx'), may hold values from -7 to 7, as said below
- head_weights: bfloat16 [4096, 64], P('ctx', 'head'), may hold values from 0.019897461 to 0.25
- row_weight: float32 [4096], P('ctx'), may hold values from 4096 to 16384
- block_offsets: int32 [16], replicated, may hold values from 126976 to 130816, as said below
Outputs:
- query_grads: float32 [4096, 64, 128], P('ctx', 'head')
- key_grads: float32 [4096, 128], P(('ctx', 'head'))
The draws below stay inside these ranges and needn't reach their ends.
Inputs may be any that keep to these rules, and one draw needn't show every extreme that they name: block_offsets is 126976 plus 256 times a permutation of 0 to 15, so the window covers the last 4096 positions of the context. `index_queries`: every entry is a multiple of 1/8. `index_keys`: every entry is a multiple of 1/8.
All inputs are finite; a program needn't handle non-finite values.
Results may differ from the reference program's by a relative error of at most 0.0029.
Values may be sent and summed in bfloat16 or wider, within the bound.
No kernel may reach another device: no remote copies, remote signals or barrier semaphores. Data moves between devices by JAX's collectives and lax.ppermute only.
A program may use at most 128 MiB of HBM per device.

```python
import math
import jax
import jax.numpy as jnp
from jax import lax

HEADS = 128
IHEADS = 64
IDIM = 128
LATENT = 576
TOK_DEV = 256
CONTEXT = 131072
BLOCKS = 16
TOKENS = 4096


def on_grid(values):
    return jnp.clip(jnp.floor(values * 8.0 + 0.5) / 8.0, -7.0, 7.0)


def key_table(key):
    raw = on_grid(jax.random.normal(jax.random.fold_in(key, 3), (TOKENS, IDIM), jnp.float32))
    return raw


def draw_index_keys(key, part):
    return key_table(key).astype(jnp.bfloat16)


def draw_index_queries(key, part):
    raw = on_grid(jax.random.normal(jax.random.fold_in(key, 5), (TOKENS, IHEADS, IDIM), jnp.float32))
    return raw.astype(jnp.bfloat16)


def draw_block_offsets(key, part):
    start = CONTEXT - TOKENS
    order = jax.random.permutation(jax.random.fold_in(key, 2), BLOCKS)
    return (start + TOK_DEV * order).astype(jnp.int32)


def shard_levels(own_key, shape, split, smallest, high):
    gain = 1.0
    for position, parts in split:
        steps = jax.random.uniform(jax.random.fold_in(jax.random.fold_in(own_key, 6), position), (parts,), jnp.float32, smallest / len(split), high / len(split))
        gain = gain * jnp.repeat(jnp.exp(steps), shape[position] // parts).reshape((-1,) + (1,) * (len(shape) - 1 - position))
    return gain


def scatter_about(key, shape, scale, bound, cuts=(), kind=jnp.bfloat16):
    values = jax.random.normal(key, shape, jnp.float32) * scale
    if len(cuts) > 0:
        values = shard_levels(key, shape, cuts, -0.22, 0.18) * values
    return jnp.clip(values, min=-bound, max=bound).astype(kind)


def setup_inputs(seed: int = 0) -> dict:
    streams_of = jax.random.split(jax.random.key(seed), 9)
    main_queries = scatter_about(streams_of[0], (TOKENS, HEADS, LATENT), 1.0, 6.0, ((0, 16), (1, 8)))
    latents = scatter_about(streams_of[1], (TOKENS, LATENT), 1.0, 6.0, ((0, 16),))
    saved_lse = jnp.clip(9.0 + 3.0 * jax.random.uniform(streams_of[2], (TOKENS, HEADS), jnp.float32) ** shard_levels(streams_of[2], (TOKENS, HEADS), ((0, 16), (1, 8)), -0.2, 0.2), 9.0, 12.0)
    index_queries = draw_index_queries(jax.random.fold_in(streams_of[8], 71), 0)
    index_keys = draw_index_keys(jax.random.fold_in(streams_of[8], 71), 0)
    head_weights = jnp.clip(0.019897461 + 0.23010254 * jax.random.uniform(streams_of[5], (TOKENS, IHEADS), jnp.float32) ** shard_levels(streams_of[5], (TOKENS, IHEADS), ((0, 16), (1, 8)), -0.2, 0.2), 0.019897461, 0.25).astype(jnp.bfloat16)
    row_weight = jnp.clip(jnp.exp(math.log(16384.0) - 1.3862944 * jax.random.uniform(streams_of[6], (TOKENS,), jnp.float32) ** shard_levels(streams_of[6], (TOKENS,), ((0, 16),), -0.2, 0.2)), 4096.0, 16384.0)
    block_offsets = draw_block_offsets(jax.random.fold_in(streams_of[8], 71), 0)
    return dict(main_queries=main_queries, latents=latents, saved_lse=saved_lse, index_queries=index_queries, index_keys=index_keys, head_weights=head_weights, row_weight=row_weight, block_offsets=block_offsets)


score_scale = 192.0 ** -0.5


def reference(main_queries, latents, saved_lse, index_queries, index_keys, head_weights, row_weight, block_offsets):
    local = jnp.arange(TOK_DEV, dtype=jnp.int32)
    pos = (jnp.repeat(block_offsets, TOK_DEV) + jnp.tile(local, BLOCKS)).astype(jnp.int32)
    iscale = IDIM ** -0.5
    qrows = math.gcd(TOKENS, 256)
    hgroup = math.gcd(HEADS, 16)
    groups = HEADS // hgroup

    def prob_rows(index):
        start = (index * qrows).astype(jnp.int32)
        qblock = lax.dynamic_slice_in_dim(main_queries, start, qrows, 0)
        lblock = lax.dynamic_slice_in_dim(saved_lse, start, qrows, 0)
        qpos = lax.dynamic_slice_in_dim(pos, start, qrows, 0)
        qgroups = qblock.reshape(qrows, groups, hgroup, LATENT).transpose(1, 0, 2, 3)
        lgroups = lblock.reshape(qrows, groups, hgroup).transpose(1, 0, 2)

        def head_step(total, inputs):
            qhead, lhead = inputs
            scores = jnp.dot(qhead.reshape(qrows * hgroup, LATENT), latents.T, preferred_element_type=jnp.float32)
            scores = scores.reshape(qrows, hgroup, TOKENS)
            return total + jnp.sum(jnp.exp(scores * score_scale - lhead[:, :, None]), axis=1), None

        total, _ = lax.scan(head_step, jnp.zeros((qrows, TOKENS), jnp.float32), (qgroups, lgroups))
        return jnp.where(pos[None, :] <= qpos[:, None], total, jnp.float32(0.0))

    mass = lax.map(prob_rows, jnp.arange(TOKENS // qrows, dtype=jnp.int32)).reshape(TOKENS, TOKENS)
    rblock = math.gcd(TOKENS, 64)
    keys_wide = index_keys.astype(jnp.float32)

    def index_step(kgrad, index):
        start = (index * rblock).astype(jnp.int32)
        queries = lax.dynamic_slice_in_dim(index_queries, start, rblock, 0)
        weights = lax.dynamic_slice_in_dim(head_weights, start, rblock, 0).astype(jnp.float32)
        lossw = lax.dynamic_slice_in_dim(row_weight, start, rblock, 0)
        qpos = lax.dynamic_slice_in_dim(pos, start, rblock, 0)
        raw = lax.dynamic_slice_in_dim(mass, start, rblock, 0)
        allowed = pos[None, :] <= qpos[:, None]
        target = raw / jnp.sum(raw, axis=1, keepdims=True)
        dots = jnp.einsum('rjd,sd->rjs', queries.astype(jnp.float32), keys_wide)
        logit = jnp.sum(jnp.maximum(dots, 0.0) * weights[:, :, None], axis=1) * iscale
        masked = jnp.where(allowed, logit, jnp.float32(-1e30))
        expo = jnp.where(allowed, jnp.exp(masked - jnp.max(masked, axis=1, keepdims=True)), jnp.float32(0.0))
        prob = expo / jnp.sum(expo, axis=1, keepdims=True)
        grad = lossw[:, None] * (prob - target)
        coef = jnp.where(dots > 0, grad[:, None, :] * weights[:, :, None], jnp.float32(0.0)).astype(jnp.bfloat16)
        coef = lax.optimization_barrier(coef).astype(jnp.float32)
        qgrad = jnp.einsum('rjs,sd->rjd', coef, keys_wide) * iscale
        kgrad = kgrad + jnp.einsum('rjs,rjd->sd', coef, queries.astype(jnp.float32)) * iscale
        return kgrad, qgrad

    kgrad, qgrad = lax.scan(index_step, jnp.zeros((TOKENS, IDIM), jnp.float32), jnp.arange(TOKENS // rblock, dtype=jnp.int32))
    return qgrad.reshape(TOKENS, IHEADS, IDIM), kgrad
```

```python
import functools

import jax
import jax.numpy as jnp
from jax import lax
from jax.experimental import pallas as pl
from jax.experimental.pallas import tpu as pltpu
from jax.sharding import Mesh
from jax.sharding import PartitionSpec as P

CTX = ("ctx_0", "ctx_1", "ctx_2")
HEAD = ("head_0", "head_1")
ALL = CTX + HEAD

ROWS = 256
LATENT = 576
IDIM = 128
HEADS_DEV = 16
PEERS = 8
SHARE = ROWS // PEERS
BLOCKS = 16
TOTAL = BLOCKS * ROWS
PAD = 16
LOG2E = 1.4426950408889634
SCORE = 192.0 ** -0.5
ISCALE = IDIM ** -0.5
VMEM = 48 * 2**20

ORDER = (
    (0, 0, 0), (0, 0, 1),
    (1, 0, 0), (0, 3, 0), (0, 1, 0), (1, 0, 1), (0, 3, 1), (0, 1, 1),
    (1, 3, 0), (1, 1, 0), (0, 2, 0), (1, 3, 1), (1, 1, 1), (0, 2, 1),
    (1, 2, 0), (1, 2, 1),
)


def mass_kernel(first, count, hstep, ids, table, q_ref, lse_ref, *refs):
    blocks, out_ref, acc = refs[:count], refs[count], refs[count + 1]
    step = pl.program_id(0)

    @pl.when(step == 0)
    def _():
        acc[...] = jnp.zeros_like(acc)

    for b in range(count):
        lat = blocks[b][:, IDIM : IDIM + LATENT]
        rows = slice(b * ROWS, (b + 1) * ROWS)
        part = None
        for i in range(hstep):
            s = jnp.dot(lat, q_ref[i], preferred_element_type=jnp.float32)
            lse = lse_ref[pl.ds(step * hstep + i, 1), :] * jnp.float32(LOG2E)
            e = jnp.exp2(s * jnp.float32(SCORE * LOG2E) - lse)
            part = e if part is None else part + e
        acc[rows, :] += part

    @pl.when(step == pl.num_programs(0) - 1)
    def _():
        q_pos = table[ids[0]] + lax.broadcasted_iota(jnp.int32, (ROWS, ROWS), 0)
        for b in range(count):
            k_pos = table[ids[first + b]] + lax.broadcasted_iota(jnp.int32, (ROWS, ROWS), 1)
            rows = slice(b * ROWS, (b + 1) * ROWS)
            mass = jnp.where(k_pos <= q_pos, acc[rows, :].T, jnp.float32(0.0))
            out_ref[:, rows] = mass.astype(jnp.bfloat16)


def mass_call(ids, table, q_t, lse_t, blocks, first, hstep=4):
    count = len(blocks)
    width = blocks[0].shape[1]
    return pl.pallas_call(
        functools.partial(mass_kernel, first, count, hstep),
        out_shape=jax.ShapeDtypeStruct((ROWS, count * ROWS), jnp.bfloat16),
        grid_spec=pltpu.PrefetchScalarGridSpec(
            num_scalar_prefetch=2,
            grid=(HEADS_DEV // hstep,),
            in_specs=[
                pl.BlockSpec((hstep, LATENT, ROWS), lambda h, *_: (h, 0, 0)),
                pl.BlockSpec((HEADS_DEV, ROWS), lambda h, *_: (0, 0)),
            ]
            + [pl.BlockSpec((ROWS, width), lambda h, *_: (0, 0))] * count,
            out_specs=pl.BlockSpec((ROWS, count * ROWS), lambda h, *_: (0, 0)),
            scratch_shapes=[pltpu.VMEM((count * ROWS, ROWS), jnp.float32)],
        ),
        compiler_params=pltpu.CompilerParams(vmem_limit_bytes=VMEM),
        cost_estimate=pl.CostEstimate(
            flops=2 * HEADS_DEV * ROWS * ROWS * count * LATENT * 4 // 3,
            bytes_accessed=HEADS_DEV * ROWS * LATENT * 2 + count * ROWS * (width + ROWS) * 2,
            transcendentals=HEADS_DEV * ROWS * ROWS * count,
        ),
        name="mass_%d" % first,
    )(ids, table, q_t, lse_t, *blocks)


def logit_kernel(qw_ref, *refs):
    blocks = refs[:BLOCKS]
    logit_ref, keys_ref, wide_ref = refs[BLOCKS:]
    for b in range(BLOCKS):
        keys_ref[b * ROWS : (b + 1) * ROWS, :] = blocks[b][...]
    for h in range(PEERS):
        w = qw_ref[h, ROWS : ROWS + PAD, :].astype(jnp.float32)
        for i in range(2):
            wide_ref[h, i * IDIM : (i + 1) * IDIM, :] = jnp.broadcast_to(
                w[i : i + 1, :], (IDIM, IDIM)
            ).T

    @pl.loop(0, BLOCKS)
    def _(b):
        keys = keys_ref[pl.ds(pl.multiple_of(b * ROWS, ROWS), ROWS), :]
        acc = [None, None]
        for h in range(PEERS):
            dots = lax.dot_general(
                qw_ref[h, :ROWS, :], keys, (((1,), (1,)), ((), ())),
                preferred_element_type=jnp.float32,
            )
            w = wide_ref[h]
            for i in range(2):
                y = jnp.maximum(dots[:, i * IDIM : (i + 1) * IDIM], 0.0) * w
                acc[i] = y if acc[i] is None else acc[i] + y
        for i in range(2):
            logit_ref[:, pl.ds(pl.multiple_of(b * ROWS + i * IDIM, IDIM), IDIM)] = jnp.sum(
                acc[i].reshape(SHARE, PEERS, IDIM), axis=1
            )


def logit_call(qw, blocks):
    return pl.pallas_call(
        logit_kernel,
        out_shape=(
            jax.ShapeDtypeStruct((SHARE, TOTAL), jnp.float32),
            jax.ShapeDtypeStruct((TOTAL, IDIM), jnp.bfloat16),
            jax.ShapeDtypeStruct((PEERS, ROWS, IDIM), jnp.float32),
        ),
        grid=(1,),
        in_specs=[pl.BlockSpec(qw.shape, lambda i: (0, 0, 0))]
        + [pl.BlockSpec((ROWS, IDIM), lambda i: (0, 0))] * BLOCKS,
        out_specs=(
            pl.BlockSpec((SHARE, TOTAL), lambda i: (0, 0)),
            pl.BlockSpec((TOTAL, IDIM), lambda i: (0, 0)),
            pl.BlockSpec((PEERS, ROWS, IDIM), lambda i: (0, 0, 0)),
        ),
        compiler_params=pltpu.CompilerParams(vmem_limit_bytes=VMEM),
        cost_estimate=pl.CostEstimate(
            flops=4 * PEERS * ROWS * TOTAL * IDIM, bytes_accessed=4 * 2**20, transcendentals=0
        ),
        name="logit",
    )(qw, *blocks)


def grad_kernel(chunks, ids, table, qw_ref, logit_ref, keys_ref, wide_ref, loss_ref, *refs):
    raws = refs[: len(chunks)]
    qgrad_ref, kterm_ref, grad, raw, q_t, acc = refs[len(chunks) :]
    sub = ids[BLOCKS] * SHARE
    q_pos = table[ids[0]] + sub + lax.broadcasted_iota(jnp.int32, (SHARE, ROWS), 0)
    peak = None
    mass = None
    start = 0
    for ref, count in zip(raws, chunks):
        for b in range(count):
            cols = slice((start + b) * ROWS, (start + b + 1) * ROWS)
            here = slice(b * ROWS, (b + 1) * ROWS)
            part = ref[0, :, here].astype(jnp.float32)
            for p in range(1, PEERS):
                part = part + ref[p, :, here].astype(jnp.float32)
            raw[:, cols] = part
            mass = part if mass is None else mass + part
            k_pos = table[ids[start + b]] + lax.broadcasted_iota(jnp.int32, (SHARE, ROWS), 1)
            masked = jnp.where(
                k_pos <= q_pos, logit_ref[:, cols] * jnp.float32(ISCALE), jnp.float32(-1e30)
            )
            grad[:, cols] = masked
            peak = masked if peak is None else jnp.maximum(peak, masked)
        start += count
    peak = jnp.max(peak, axis=1, keepdims=True)
    loss = loss_ref[:, :1]
    mass = loss / jnp.sum(mass, axis=1, keepdims=True)
    total = None
    for b in range(BLOCKS):
        cols = slice(b * ROWS, (b + 1) * ROWS)
        e = jnp.exp(grad[:, cols] - peak)
        grad[:, cols] = e
        total = e if total is None else total + e
    total = loss / jnp.sum(total, axis=1, keepdims=True)
    for b in range(BLOCKS):
        cols = slice(b * ROWS, (b + 1) * ROWS)
        grad[:, cols] = grad[:, cols] * total - raw[:, cols] * mass
    for h in range(PEERS):
        q_t[h] = qw_ref[h, :ROWS, :].T
    acc[...] = jnp.zeros_like(acc)

    @pl.loop(0, BLOCKS)
    def _(b):
        rows = pl.ds(pl.multiple_of(b * ROWS, ROWS), ROWS)
        keys = keys_ref[rows, :]
        g = grad[:, rows]
        g = jnp.broadcast_to(g[:, None, :], (SHARE, PEERS, ROWS)).reshape(ROWS, ROWS)
        kterm = None
        for h in range(PEERS):
            dots = lax.dot_general(
                qw_ref[h, :ROWS, :], keys, (((1,), (1,)), ((), ())),
                preferred_element_type=jnp.float32,
            )
            w = wide_ref[h]
            w = jnp.concatenate([w, w], axis=1)
            coef = jnp.where(dots > 0, g * w, jnp.float32(0.0)).astype(jnp.bfloat16)
            acc[h] += jnp.dot(coef, keys, preferred_element_type=jnp.float32)
            part = jnp.dot(q_t[h], coef, preferred_element_type=jnp.float32)
            kterm = part if kterm is None else kterm + part
        kterm = (kterm * jnp.float32(ISCALE)).T
        place = pl.ds(pl.multiple_of(ids[b] * ROWS, ROWS), ROWS)
        kterm_ref[place, :] = kterm.astype(kterm_ref.dtype)

    qgrad_ref[...] = (acc[...] * jnp.float32(ISCALE)).astype(qgrad_ref.dtype)


def grad_call(ids, table, qw, logit, keys, wide, loss, raws):
    chunks = tuple(r.shape[2] // ROWS for r in raws)
    whole = lambda a: pl.BlockSpec(a.shape, lambda i, *_, n=a.ndim: (0,) * n)
    operands = (qw, logit, keys, wide, loss) + tuple(raws)
    return pl.pallas_call(
        functools.partial(grad_kernel, chunks),
        out_shape=(
            jax.ShapeDtypeStruct((PEERS, ROWS, IDIM), jnp.bfloat16),
            jax.ShapeDtypeStruct((TOTAL, IDIM), jnp.bfloat16),
        ),
        grid_spec=pltpu.PrefetchScalarGridSpec(
            num_scalar_prefetch=2,
            grid=(1,),
            in_specs=[whole(a) for a in operands],
            out_specs=(
                pl.BlockSpec((PEERS, ROWS, IDIM), lambda i, *_: (0, 0, 0)),
                pl.BlockSpec((TOTAL, IDIM), lambda i, *_: (0, 0)),
            ),
            scratch_shapes=[
                pltpu.VMEM((SHARE, TOTAL), jnp.float32),
                pltpu.VMEM((SHARE, TOTAL), jnp.float32),
                pltpu.VMEM((PEERS, IDIM, ROWS), jnp.bfloat16),
                pltpu.VMEM((PEERS, ROWS, IDIM), jnp.float32),
            ],
        ),
        compiler_params=pltpu.CompilerParams(vmem_limit_bytes=VMEM),
        cost_estimate=pl.CostEstimate(
            flops=12 * PEERS * ROWS * TOTAL * IDIM, bytes_accessed=8 * 2**20, transcendentals=0
        ),
        name="grads",
    )(ids, table, *operands)


def shift(array, axis, size, by):
    return lax.ppermute(array, axis, [(i, (i + by) % size) for i in range(size)])


def local(
    main_queries, latents, saved_lse, index_queries, index_keys, head_weights, row_weight,
    block_offsets,
):
    c0, c1, c2 = (lax.axis_index(a) for a in CTX)
    head = lax.axis_index(HEAD)
    ids = [(c0 ^ a) * 8 + ((c1 + b) & 3) * 2 + (c2 ^ c) for a, b, c in ORDER]
    ids = jnp.stack([i.astype(jnp.int32) for i in ids + [head]])

    own = jnp.concatenate([index_keys, latents], axis=1)
    core = functools.partial(shift, axis="ctx_2", size=2, by=1)
    up = functools.partial(shift, axis="ctx_1", size=4, by=1)
    down = functools.partial(shift, axis="ctx_1", size=4, by=-1)
    side = functools.partial(shift, axis="ctx_0", size=2, by=1)

    weights = head_weights.reshape(PEERS, 2, IDIM)
    weights = jnp.pad(weights, ((0, 0), (0, PAD - 2), (0, 0)))
    qw = jnp.concatenate([index_queries.reshape(PEERS, ROWS, IDIM), weights], axis=1)

    pair = core(own)
    z, yp, ym = side(own), up(own), down(own)
    pz, pyp, pym = core(z), core(yp), core(ym)
    zyp, zym, y2 = up(z), down(z), up(yp)
    pzyp, pzym, py2 = core(zyp), core(zym), core(y2)
    zy2 = down(zym)
    pzy2 = core(zy2)
    qw = lax.all_to_all(qw, HEAD, 0, 0, tiled=True)

    q_t = jnp.transpose(main_queries, (1, 2, 0))
    lse_t = saved_lse.T
    mass = functools.partial(mass_call, ids, block_offsets, q_t, lse_t)

    def exchange(parts):
        m = jnp.concatenate(parts, axis=1).reshape(PEERS, SHARE, -1)
        return lax.all_to_all(m, HEAD, 0, 0, tiled=True)

    raw_0 = exchange([mass([own, pair], 0), mass([z, yp, ym, pz, pyp, pym], 2)])
    raw_1 = exchange([mass([zyp, zym, y2, pzyp, pzym, py2], 8), mass([zy2, pzy2], 14)])

    blocks = [own, pair, z, yp, ym, pz, pyp, pym, zyp, zym, y2, pzyp, pzym, py2, zy2, pzy2]
    logit, keys, wide = logit_call(qw, blocks)
    loss = lax.dynamic_slice_in_dim(row_weight, head * SHARE, SHARE, 0)
    loss = jnp.broadcast_to(loss[:, None], (SHARE, IDIM))
    qgrad, kterm = grad_call(ids, block_offsets, qw, logit, keys, wide, loss, (raw_0, raw_1))

    qgrad = lax.all_to_all(qgrad, HEAD, 0, 0, tiled=True)
    query_grads = qgrad.reshape(ROWS, PEERS, IDIM).astype(jnp.float32)
    kterm = lax.all_to_all(kterm.reshape(BLOCKS * PEERS, SHARE, IDIM), ALL, 0, 0, tiled=True)
    key_grads = jnp.sum(kterm.astype(jnp.float32), axis=0)
    return query_grads, key_grads


def solution(mesh):
    torus = Mesh(mesh.devices.reshape(2, 4, 2, 4, 2), ALL)
    placed = (
        P(CTX, HEAD, None), P(CTX, None), P(CTX, HEAD), P(CTX, HEAD, None), P(CTX, None),
        P(CTX, HEAD), P(CTX), P(),
    )
    return jax.shard_map(
        local,
        mesh=torus,
        in_specs=placed,
        out_specs=(P(CTX, HEAD, None), P(ALL, None)),
        check_vma=False,
    )
```

```python
import functools

import jax
import jax.numpy as jnp
from jax import lax
from jax.experimental import pallas as pl
from jax.experimental.pallas import tpu as pltpu
from jax.sharding import Mesh
from jax.sharding import PartitionSpec as P

CTX = ("ctx_0", "ctx_1", "ctx_2")
HEAD = ("head_0", "head_1")
ALL = CTX + HEAD

ROWS = 256
LATENT = 576
IDIM = 128
HEADS_DEV = 16
PEERS = 8
SHARE = ROWS // PEERS
BLOCKS = 16
TOTAL = BLOCKS * ROWS
PAD = 16
LOG2E = 1.4426950408889634
SCORE = 192.0 ** -0.5
ISCALE = IDIM ** -0.5
WIDE = 1024
MIB = 2**20

ORDER = (
    (0, 0, 0), (0, 0, 1),
    (1, 0, 0), (0, 3, 0), (0, 1, 0), (1, 0, 1), (0, 3, 1), (0, 1, 1),
    (1, 3, 0), (1, 1, 0), (0, 2, 0), (1, 3, 1), (1, 1, 1), (0, 2, 1), (1, 2, 0), (1, 2, 1),
)

SORTED = tuple(k for p in range(2) for k in range(BLOCKS) if ORDER[k][2] == p)
PLACE = tuple(SORTED.index(k) for k in range(BLOCKS))
HALF = TOTAL // 2
VMEM = pltpu.VMEM


def mass_kernel(first, count, carried, hstep, ids, table, q_ref, lse_ref, *refs):
    blocks, extra = refs[:count], refs[count : count + carried]
    out_ref, keys_ref, acc = refs[count + carried :]
    step = pl.program_id(0)

    @pl.when(step == 0)
    def _():
        acc[...] = jnp.zeros_like(acc)
        for b in range(count):
            keys_ref[b * ROWS : (b + 1) * ROWS, :] = blocks[b][:, :IDIM]

    for b in range(count):
        lat = blocks[b][:, IDIM : IDIM + LATENT]
        rows = slice(b * ROWS, (b + 1) * ROWS)
        part = None
        for i in range(hstep):
            s = jnp.dot(lat, q_ref[step * hstep + i], preferred_element_type=jnp.float32)
            lse = lse_ref[pl.ds(step * hstep + i, 1), :] * jnp.float32(LOG2E)
            e = jnp.exp2(s * jnp.float32(SCORE * LOG2E) - lse)
            part = e if part is None else part + e
        acc[rows, :] += part

    @pl.when(step == pl.num_programs(0) - 1)
    def _():
        place = 0
        for ref in extra:
            size = ref.shape[1]
            out_ref[:, place : place + size, :] = ref[...]
            place += size
        q_pos = table[ids[0]] + lax.broadcasted_iota(jnp.int32, (ROWS, ROWS), 0)
        for b in range(count):
            k_pos = table[ids[first + b]] + lax.broadcasted_iota(jnp.int32, (ROWS, ROWS), 1)
            mass = acc[b * ROWS : (b + 1) * ROWS, :].T
            mass = jnp.where(k_pos <= q_pos, mass, jnp.float32(0.0)).astype(jnp.bfloat16)
            for i in range(2):
                half = mass[:, i * IDIM : (i + 1) * IDIM].reshape(PEERS, SHARE, IDIM)
                out_ref[:, place : place + SHARE, :] = half
                place += SHARE


def mass_call(ids, table, q_t, lse_t, blocks, first, extra=(), hstep=4):
    count = len(blocks)
    width = blocks[0].shape[1]
    rows = sum(e.shape[1] for e in extra) + count * 2 * SHARE
    return pl.pallas_call(
        functools.partial(mass_kernel, first, count, len(extra), hstep),
        out_shape=(
            jax.ShapeDtypeStruct((PEERS, rows, IDIM), jnp.bfloat16),
            jax.ShapeDtypeStruct((count * ROWS, IDIM), jnp.bfloat16),
        ),
        grid_spec=pltpu.PrefetchScalarGridSpec(
            num_scalar_prefetch=2,
            grid=(HEADS_DEV // hstep,),
            in_specs=[
                pl.BlockSpec(memory_space=VMEM),
                pl.BlockSpec((HEADS_DEV, ROWS), lambda h, *_: (0, 0)),
            ]
            + [pl.BlockSpec((ROWS, width), lambda h, *_: (0, 0))] * count
            + [pl.BlockSpec(e.shape, lambda h, *_: (0, 0, 0)) for e in extra],
            out_specs=(
                pl.BlockSpec((PEERS, rows, IDIM), lambda h, *_: (0, 0, 0)),
                pl.BlockSpec((count * ROWS, IDIM), lambda h, *_: (0, 0)),
            ),
            scratch_shapes=[pltpu.VMEM((count * ROWS, ROWS), jnp.float32)],
        ),
        compiler_params=pltpu.CompilerParams(vmem_limit_bytes=24 * MIB),
        cost_estimate=pl.CostEstimate(
            flops=2 * HEADS_DEV * ROWS * ROWS * count * LATENT * 4 // 3,
            bytes_accessed=HEADS_DEV * ROWS * LATENT * 2 + count * ROWS * (width + ROWS) * 2,
            transcendentals=HEADS_DEV * ROWS * ROWS * count,
        ),
        name="mass_%d" % first,
    )(ids, table, q_t, lse_t, *blocks, *extra)


def prob_kernel(ids, table, loss_ref, qw_ref, *refs):
    pieces = refs[:-5]
    prob_ref, keys_ref, gates_ref, wide, logit = refs[-5:]
    step = pl.program_id(0)

    @pl.when(step == 0)
    def _():
        done = 0
        for piece in pieces:
            for start in range(0, piece.shape[0], ROWS):
                place = PLACE[done] * ROWS
                keys_ref[place : place + ROWS, :] = piece[start : start + ROWS, :]
                done += 1
        for h in range(PEERS):
            w = qw_ref[h, ROWS : ROWS + PAD, :].astype(jnp.float32)
            for i in range(2):
                wide[h, i * IDIM : (i + 1) * IDIM, :] = jnp.broadcast_to(
                    w[i : i + 1, :], (IDIM, IDIM)
                ).T

    count = WIDE // IDIM
    start = pl.multiple_of(step * WIDE, WIDE)
    keys = keys_ref[pl.ds(start, WIDE), :]
    acc = [None] * count
    for h in range(PEERS):
        dots = lax.dot_general(
            qw_ref[h, :ROWS, :], keys, (((1,), (1,)), ((), ())),
            preferred_element_type=jnp.float32,
        )
        w = wide[h]
        rows = slice(h * ROWS, (h + 1) * ROWS)
        for i in range(count):
            cols = slice(i * IDIM, (i + 1) * IDIM)
            gate = jnp.where(dots[:, cols] > 0, w, jnp.float32(0.0))
            gates_ref[rows, cols] = gate.astype(jnp.bfloat16)
            y = gate * dots[:, cols]
            acc[i] = y if acc[i] is None else acc[i] + y
    for i in range(count):
        cols = pl.ds(pl.multiple_of(start + i * IDIM, IDIM), IDIM)
        logit[:, cols] = jnp.sum(acc[i].reshape(SHARE, PEERS, IDIM), axis=1)

    @pl.when(step == pl.num_programs(0) - 1)
    def _():
        sub = ids[BLOCKS] * SHARE
        q_pos = table[ids[0]] + sub + lax.broadcasted_iota(jnp.int32, (SHARE, ROWS), 0)
        lane = lax.broadcasted_iota(jnp.int32, (SHARE, ROWS), 1)
        peak = None
        for b in range(BLOCKS):
            cols = slice(b * ROWS, (b + 1) * ROWS)
            masked = jnp.where(
                table[ids[SORTED[b]]] + lane <= q_pos,
                logit[:, cols] * jnp.float32(ISCALE),
                jnp.float32(-1e30),
            )
            logit[:, cols] = masked
            peak = masked if peak is None else jnp.maximum(peak, masked)
        peak = jnp.max(peak, axis=1, keepdims=True)
        total = None
        for b in range(BLOCKS):
            cols = slice(b * ROWS, (b + 1) * ROWS)
            e = jnp.exp(logit[:, cols] - peak)
            logit[:, cols] = e
            total = e if total is None else total + e
        total = loss_ref[:, :1] / jnp.sum(total, axis=1, keepdims=True)
        for b in range(BLOCKS):
            cols = slice(b * ROWS, (b + 1) * ROWS)
            prob_ref[:, cols] = logit[:, cols] * total


def prob_call(ids, table, loss, qw, pieces):
    return pl.pallas_call(
        prob_kernel,
        out_shape=(
            jax.ShapeDtypeStruct((SHARE, TOTAL), jnp.float32),
            jax.ShapeDtypeStruct((TOTAL, IDIM), jnp.bfloat16),
            jax.ShapeDtypeStruct((PEERS * ROWS, TOTAL), jnp.bfloat16),
        ),
        grid_spec=pltpu.PrefetchScalarGridSpec(
            num_scalar_prefetch=2,
            grid=(TOTAL // WIDE,),
            in_specs=[
                pl.BlockSpec((SHARE, IDIM), lambda i, *_: (0, 0)),
                pl.BlockSpec((PEERS, ROWS + PAD, IDIM), lambda i, *_: (0, 0, 0)),
            ]
            + [pl.BlockSpec(p.shape, lambda i, *_: (0, 0)) for p in pieces],
            out_specs=(
                pl.BlockSpec((SHARE, TOTAL), lambda i, *_: (0, 0)),
                pl.BlockSpec((TOTAL, IDIM), lambda i, *_: (0, 0)),
                pl.BlockSpec((PEERS * ROWS, WIDE), lambda i, *_: (0, i)),
            ),
            scratch_shapes=[
                pltpu.VMEM((PEERS, ROWS, IDIM), jnp.float32),
                pltpu.VMEM((SHARE, TOTAL), jnp.float32),
            ],
        ),
        compiler_params=pltpu.CompilerParams(vmem_limit_bytes=60 * MIB),
        cost_estimate=pl.CostEstimate(
            flops=8 * PEERS * ROWS * TOTAL * IDIM, bytes_accessed=20 * MIB, transcendentals=0
        ),
        name="probs",
    )(ids, table, loss, qw, *pieces)


def coef_tile(coefs, g, gates_ref):
    g = jnp.broadcast_to(g[:, None, :], (SHARE, PEERS, WIDE)).reshape(ROWS, WIDE)
    for h in range(PEERS):
        part = slice(h * ROWS, (h + 1) * ROWS)
        coefs[part, :] = (g * gates_ref[part, :].astype(jnp.float32)).astype(jnp.bfloat16)


def kterm_tile(coefs, q_t):
    kterm = jnp.dot(q_t[...], coefs[...], preferred_element_type=jnp.float32)
    return (kterm * jnp.float32(ISCALE)).T


def grad_kernel(starts, ids, prob_ref, keys_ref, gates_ref, loss_ref, *refs):
    raws = refs[: len(starts)]
    qgrad_ref, kterm_ref, half_ref, q_t, grad, acc, coefs = refs[len(starts) :]
    qw_ref = raws[0]
    step = pl.program_id(0)

    @pl.when(step == 0)
    def _():
        mass = None
        done = 0
        for ref, start in zip(raws, starts):
            for place in range(start, ref.shape[1], SHARE):
                part = ref[0, place : place + SHARE, :].astype(jnp.float32)
                for p in range(1, PEERS):
                    part = part + ref[p, place : place + SHARE, :].astype(jnp.float32)
                col = (PLACE[done // 2] * 2 + done % 2) * IDIM
                grad[:, col : col + IDIM] = part
                mass = part if mass is None else mass + part
                done += 1
        mass = loss_ref[:, :1] / jnp.sum(mass, axis=1, keepdims=True)
        for b in range(BLOCKS):
            cols = slice(b * ROWS, (b + 1) * ROWS)
            grad[:, cols] = prob_ref[:, cols] - grad[:, cols] * mass
        half_ref[...] = grad[:, :HALF]
        for h in range(PEERS):
            q_t[:, h * ROWS : (h + 1) * ROWS] = qw_ref[h, :ROWS, :].T
        acc[...] = jnp.zeros_like(acc)

    rows = pl.ds(pl.multiple_of(step * WIDE, WIDE), WIDE)
    coef_tile(coefs, grad[:, rows], gates_ref)
    acc[...] += jnp.dot(coefs[...], keys_ref[rows, :], preferred_element_type=jnp.float32)
    for tile in range(HALF // WIDE, TOTAL // WIDE):

        @pl.when(step == tile)
        def _():
            kterm = kterm_tile(coefs, q_t)
            for i in range(WIDE // ROWS):
                place = ids[SORTED[tile * (WIDE // ROWS) + i]] >> 1
                place = pl.ds(pl.multiple_of(place * ROWS, ROWS), ROWS)
                kterm_ref[place, :] = kterm[i * ROWS : (i + 1) * ROWS, :]

    @pl.when(step == pl.num_programs(0) - 1)
    def _():
        for h in range(PEERS):
            qgrad = acc[h * ROWS : (h + 1) * ROWS, :] * jnp.float32(ISCALE)
            qgrad_ref[h] = qgrad.astype(jnp.bfloat16)


def whole(a):
    return pl.BlockSpec(a.shape, lambda i, *_: (0,) * len(a.shape))


GATES = pl.BlockSpec((PEERS * ROWS, WIDE), lambda i, *_: (0, i))


def grad_call(ids, prob, keys, gates, loss, raws, starts):
    out_shape = (
        jax.ShapeDtypeStruct((PEERS, ROWS, IDIM), jnp.bfloat16),
        jax.ShapeDtypeStruct((HALF, IDIM), jnp.float32),
        jax.ShapeDtypeStruct((SHARE, HALF), jnp.float32),
        jax.ShapeDtypeStruct((IDIM, PEERS * ROWS), jnp.bfloat16),
    )
    return pl.pallas_call(
        functools.partial(grad_kernel, starts),
        out_shape=out_shape,
        grid_spec=pltpu.PrefetchScalarGridSpec(
            num_scalar_prefetch=1,
            grid=(TOTAL // WIDE,),
            in_specs=[whole(prob), whole(keys), GATES, whole(loss)] + [whole(r) for r in raws],
            out_specs=tuple(whole(o) for o in out_shape),
            scratch_shapes=[
                pltpu.VMEM((SHARE, TOTAL), jnp.float32),
                pltpu.VMEM((PEERS * ROWS, IDIM), jnp.float32),
                pltpu.VMEM((PEERS * ROWS, WIDE), jnp.bfloat16),
            ],
        ),
        compiler_params=pltpu.CompilerParams(vmem_limit_bytes=60 * MIB),
        cost_estimate=pl.CostEstimate(
            flops=6 * PEERS * ROWS * TOTAL * IDIM, bytes_accessed=26 * MIB, transcendentals=0
        ),
        name="grads",
    )(ids, prob, keys, gates, loss, *raws)


def kterm_kernel(ids, half_ref, gates_ref, q_t, other_ref, out_ref, coefs):
    step = pl.program_id(0)
    for tile in range(HALF // WIDE):

        @pl.when(step == tile)
        def _():
            coef_tile(coefs, half_ref[:, tile * WIDE : (tile + 1) * WIDE], gates_ref)
            kterm = kterm_tile(coefs, q_t)
            for i in range(WIDE // ROWS):
                place = ids[SORTED[tile * (WIDE // ROWS) + i]] >> 1
                place = pl.ds(pl.multiple_of(place * ROWS, ROWS), ROWS)
                part = kterm[i * ROWS : (i + 1) * ROWS, :] + other_ref[place, :]
                out_ref[place, :] = part.astype(jnp.bfloat16)


def kterm_call(ids, half, gates, q_t, other):
    out = jax.ShapeDtypeStruct((HALF, IDIM), jnp.bfloat16)
    return pl.pallas_call(
        kterm_kernel,
        out_shape=out,
        grid_spec=pltpu.PrefetchScalarGridSpec(
            num_scalar_prefetch=1,
            grid=(HALF // WIDE,),
            in_specs=[whole(half), GATES, whole(q_t), whole(other)],
            out_specs=whole(out),
            scratch_shapes=[pltpu.VMEM((PEERS * ROWS, WIDE), jnp.bfloat16)],
        ),
        compiler_params=pltpu.CompilerParams(vmem_limit_bytes=60 * MIB),
        cost_estimate=pl.CostEstimate(
            flops=2 * PEERS * ROWS * TOTAL * IDIM, bytes_accessed=12 * MIB, transcendentals=0
        ),
        name="kterms",
    )(ids, half, gates, q_t, other)


def shift(array, axis, size, by):
    return lax.ppermute(array, axis, [(i, (i + by) % size) for i in range(size)])


def local(
    main_queries, latents, saved_lse, index_queries, index_keys, head_weights, row_weight,
    block_offsets,
):
    c0, c1, c2 = (lax.axis_index(a) for a in CTX)
    head = lax.axis_index(HEAD)
    ids = [(c0 ^ a) * 8 + ((c1 + b) & 3) * 2 + (c2 ^ c) for a, b, c in ORDER]
    ids = jnp.stack([i.astype(jnp.int32) for i in ids + [head]])

    own = jnp.concatenate([index_keys, latents], axis=1)
    core = functools.partial(shift, axis="ctx_2", size=2, by=1)
    up = functools.partial(shift, axis="ctx_1", size=4, by=1)
    down = functools.partial(shift, axis="ctx_1", size=4, by=-1)
    side = functools.partial(shift, axis="ctx_0", size=2, by=1)

    weights = head_weights.reshape(PEERS, 2, IDIM)
    weights = jnp.pad(weights, ((0, 0), (0, PAD - 2), (0, 0)))
    qw = jnp.concatenate([index_queries.reshape(PEERS, ROWS, IDIM), weights], axis=1)

    q_t = jnp.transpose(main_queries, (1, 2, 0))
    lse_t = saved_lse.T
    loss = lax.dynamic_slice_in_dim(row_weight, head * SHARE, SHARE, 0)
    loss = jnp.broadcast_to(loss[:, None], (SHARE, IDIM))
    q_t, lse_t, loss, qw, ids = lax.optimization_barrier((q_t, lse_t, loss, qw, ids))
    mass = functools.partial(mass_call, ids, block_offsets, q_t, lse_t)

    q_t = jnp.transpose(main_queries, (1, 2, 0))
    lse_t = saved_lse.T
    loss = lax.dynamic_slice_in_dim(row_weight, head * SHARE, SHARE, 0)
    loss = jnp.broadcast_to(loss[:, None], (SHARE, IDIM))
    q_t, lse_t, loss, qw, ids = lax.optimization_barrier((q_t, lse_t, loss, qw, ids))
    mass = functools.partial(mass_call, ids, block_offsets, q_t, lse_t)

    pair = core(own)
    z, yp, ym = side(own), up(own), down(own)
    near, keys_0 = mass([own, pair], 0)
    z, yp, ym, near = lax.optimization_barrier((z, yp, ym, near))
    zyp, zym, y2 = up(z), down(z), up(yp)
    pz, pyp, pym = core(z), core(yp), core(ym)
    raw_0, keys_1 = mass([z, yp, ym, pz, pyp, pym], 2, (qw, near))
    zyp, zym, y2, raw_0 = lax.optimization_barrier((zyp, zym, y2, raw_0))
    pzyp, pzym, py2 = core(zyp), core(zym), core(y2)
    zy2, pzy2 = down(zym), up(pzyp)
    raw_0 = lax.all_to_all(raw_0, HEAD, 0, 0, tiled=True)
    raw_1, keys_2 = mass([zyp, zym, y2, pzyp, pzym, py2, zy2, pzy2], 8)
    raw_1 = lax.all_to_all(raw_1, HEAD, 0, 0, tiled=True)

    prob, keys, gates = prob_call(ids, block_offsets, loss, raw_0, (keys_0, keys_1, keys_2))
    qgrad, other, half, i_t = grad_call(
        ids, prob, keys, gates, loss, (raw_0, raw_1), (ROWS + PAD, 0)
    )
    other = core(other)
    qgrad = lax.all_to_all(qgrad, HEAD, 0, 0, tiled=True)
    kterm = kterm_call(ids, half, gates, i_t, other)
    kterm = kterm.reshape(HALF // SHARE, SHARE, IDIM)
    kterm = lax.all_to_all(kterm, CTX[:2] + HEAD, 0, 0, tiled=True)
    query_grads = qgrad.reshape(ROWS, PEERS, IDIM).astype(jnp.float32)
    key_grads = jnp.sum(kterm.astype(jnp.float32), axis=0)
    return query_grads, key_grads


def solution(mesh):
    torus = Mesh(mesh.devices.reshape(2, 4, 2, 4, 2), ALL)
    placed = (
        P(CTX, HEAD, None), P(CTX, None), P(CTX, HEAD), P(CTX, HEAD, None), P(CTX, None),
        P(CTX, HEAD), P(CTX), P(),
    )
    return jax.shard_map(
        local,
        mesh=torus,
        in_specs=placed,
        out_specs=(P(CTX, HEAD, None), P(ALL, None)),
        check_vma=False,
    )
```

```python
import functools

import jax
import jax.numpy as jnp
from jax import lax
from jax.experimental import pallas as pl
from jax.experimental.pallas import tpu as pltpu
from jax.sharding import Mesh
from jax.sharding import PartitionSpec as P

CTX = ("ctx_0", "ctx_1", "ctx_2")
HEAD = ("head_0", "head_1")
ALL = CTX + HEAD

ROWS = 256
LATENT = 576
IDIM = 128
HEADS_DEV = 16
PEERS = 8
SHARE = ROWS // PEERS
BLOCKS = 16
TOTAL = BLOCKS * ROWS
PAD = 16
LOG2E = 1.4426950408889634
SCORE = 192.0 ** -0.5
ISCALE = IDIM ** -0.5
WIDE = 1024
MIB = 2**20

ORDER = (
    (0, 0, 0), (0, 0, 1),
    (1, 0, 0), (0, 3, 0), (0, 1, 0), (1, 0, 1), (0, 3, 1), (0, 1, 1),
    (1, 3, 0), (1, 1, 0), (0, 2, 0), (1, 3, 1), (1, 1, 1), (0, 2, 1), (1, 2, 0), (1, 2, 1),
)

SORTED = tuple(k for p in range(2) for k in range(BLOCKS) if ORDER[k][2] == p)
PLACE = tuple(SORTED.index(k) for k in range(BLOCKS))
HALF = TOTAL // 2
VMEM = pltpu.VMEM


def in_hbm(array):
    return pltpu.with_memory_space_constraint(array, pltpu.HBM)


def mass_kernel(first, count, carried, hstep, ids, table, q_ref, lse_ref, *refs):
    blocks, extra = refs[:count], refs[count : count + carried]
    out_ref, keys_ref, acc = refs[count + carried :]
    step = pl.program_id(0)

    @pl.when(step == 0)
    def _():
        acc[...] = jnp.zeros_like(acc)
        for b in range(count):
            keys_ref[b * ROWS : (b + 1) * ROWS, :] = blocks[b][:, :IDIM]

    for b in range(count):
        lat = blocks[b][:, IDIM : IDIM + LATENT]
        rows = slice(b * ROWS, (b + 1) * ROWS)
        part = None
        for i in range(hstep):
            s = jnp.dot(lat, q_ref[step * hstep + i], preferred_element_type=jnp.float32)
            lse = lse_ref[pl.ds(step * hstep + i, 1), :] * jnp.float32(LOG2E)
            e = jnp.exp2(s * jnp.float32(SCORE * LOG2E) - lse)
            part = e if part is None else part + e
        acc[rows, :] += part

    @pl.when(step == pl.num_programs(0) - 1)
    def _():
        place = 0
        for ref in extra:
            size = ref.shape[1]
            out_ref[:, place : place + size, :] = ref[...]
            place += size
        q_pos = table[ids[0]] + lax.broadcasted_iota(jnp.int32, (ROWS, ROWS), 0)
        for b in range(count):
            k_pos = table[ids[first + b]] + lax.broadcasted_iota(jnp.int32, (ROWS, ROWS), 1)
            mass = acc[b * ROWS : (b + 1) * ROWS, :].T
            mass = jnp.where(k_pos <= q_pos, mass, jnp.float32(0.0)).astype(jnp.bfloat16)
            for i in range(2):
                half = mass[:, i * IDIM : (i + 1) * IDIM].reshape(PEERS, SHARE, IDIM)
                out_ref[:, place : place + SHARE, :] = half
                place += SHARE


def mass_call(ids, table, q_t, lse_t, blocks, first, extra=(), hstep=4):
    count = len(blocks)
    width = blocks[0].shape[1]
    rows = sum(e.shape[1] for e in extra) + count * 2 * SHARE
    return pl.pallas_call(
        functools.partial(mass_kernel, first, count, len(extra), hstep),
        out_shape=(
            jax.ShapeDtypeStruct((PEERS, rows, IDIM), jnp.bfloat16),
            pltpu.HBM((count * ROWS, IDIM), jnp.bfloat16),
        ),
        grid_spec=pltpu.PrefetchScalarGridSpec(
            num_scalar_prefetch=2,
            grid=(HEADS_DEV // hstep,),
            in_specs=[
                pl.BlockSpec(memory_space=VMEM),
                pl.BlockSpec((HEADS_DEV, ROWS), lambda h, *_: (0, 0)),
            ]
            + [pl.BlockSpec((ROWS, width), lambda h, *_: (0, 0))] * count
            + [pl.BlockSpec(e.shape, lambda h, *_: (0, 0, 0)) for e in extra],
            out_specs=(
                pl.BlockSpec((PEERS, rows, IDIM), lambda h, *_: (0, 0, 0)),
                pl.BlockSpec((count * ROWS, IDIM), lambda h, *_: (0, 0)),
            ),
            scratch_shapes=[pltpu.VMEM((count * ROWS, ROWS), jnp.float32)],
        ),
        compiler_params=pltpu.CompilerParams(vmem_limit_bytes=24 * MIB),
        cost_estimate=pl.CostEstimate(
            flops=2 * HEADS_DEV * ROWS * ROWS * count * LATENT * 4 // 3,
            bytes_accessed=HEADS_DEV * ROWS * LATENT * 2 + count * ROWS * (width + ROWS) * 2,
            transcendentals=HEADS_DEV * ROWS * ROWS * count,
        ),
        name="mass_%d" % first,
    )(ids, table, q_t, lse_t, *blocks, *extra)


def prob_kernel(ids, table, loss_ref, qw_ref, *refs):
    pieces = refs[:-5]
    prob_ref, keys_ref, gates_ref, wide, logit = refs[-5:]
    step = pl.program_id(0)

    @pl.when(step == 0)
    def _():
        done = 0
        for piece in pieces:
            for start in range(0, piece.shape[0], ROWS):
                place = PLACE[done] * ROWS
                keys_ref[place : place + ROWS, :] = piece[start : start + ROWS, :]
                done += 1
        for h in range(PEERS):
            w = qw_ref[h, ROWS : ROWS + PAD, :].astype(jnp.float32)
            for i in range(2):
                wide[h, i * IDIM : (i + 1) * IDIM, :] = jnp.broadcast_to(
                    w[i : i + 1, :], (IDIM, IDIM)
                ).T

    count = WIDE // IDIM
    start = pl.multiple_of(step * WIDE, WIDE)
    keys = keys_ref[pl.ds(start, WIDE), :]
    acc = [None] * count
    for h in range(PEERS):
        dots = lax.dot_general(
            qw_ref[h, :ROWS, :], keys, (((1,), (1,)), ((), ())),
            preferred_element_type=jnp.float32,
        )
        w = wide[h]
        rows = slice(h * ROWS, (h + 1) * ROWS)
        for i in range(count):
            cols = slice(i * IDIM, (i + 1) * IDIM)
            gate = jnp.where(dots[:, cols] > 0, w, jnp.float32(0.0))
            gates_ref[0, rows, cols] = gate.astype(jnp.bfloat16)
            y = gate * dots[:, cols]
            acc[i] = y if acc[i] is None else acc[i] + y
    for i in range(count):
        cols = pl.ds(pl.multiple_of(start + i * IDIM, IDIM), IDIM)
        logit[:, cols] = jnp.sum(acc[i].reshape(SHARE, PEERS, IDIM), axis=1)

    @pl.when(step == pl.num_programs(0) - 1)
    def _():
        sub = ids[BLOCKS] * SHARE
        q_pos = table[ids[0]] + sub + lax.broadcasted_iota(jnp.int32, (SHARE, ROWS), 0)
        lane = lax.broadcasted_iota(jnp.int32, (SHARE, ROWS), 1)
        peak = None
        for b in range(BLOCKS):
            cols = slice(b * ROWS, (b + 1) * ROWS)
            masked = jnp.where(
                table[ids[SORTED[b]]] + lane <= q_pos,
                logit[:, cols] * jnp.float32(ISCALE),
                jnp.float32(-1e30),
            )
            logit[:, cols] = masked
            peak = masked if peak is None else jnp.maximum(peak, masked)
        peak = jnp.max(peak, axis=1, keepdims=True)
        total = None
        for b in range(BLOCKS):
            cols = slice(b * ROWS, (b + 1) * ROWS)
            e = jnp.exp(logit[:, cols] - peak)
            logit[:, cols] = e
            total = e if total is None else total + e
        total = loss_ref[:, :1] / jnp.sum(total, axis=1, keepdims=True)
        for b in range(BLOCKS):
            cols = slice(b * ROWS, (b + 1) * ROWS)
            prob_ref[:, cols] = logit[:, cols] * total


def prob_call(ids, table, loss, qw, pieces):
    return pl.pallas_call(
        prob_kernel,
        out_shape=(
            jax.ShapeDtypeStruct((SHARE, TOTAL), jnp.float32),
            jax.ShapeDtypeStruct((TOTAL, IDIM), jnp.bfloat16),
            jax.ShapeDtypeStruct((TOTAL // WIDE, PEERS * ROWS, WIDE), jnp.bfloat16),
        ),
        grid_spec=pltpu.PrefetchScalarGridSpec(
            num_scalar_prefetch=2,
            grid=(TOTAL // WIDE,),
            in_specs=[
                pl.BlockSpec((SHARE, IDIM), lambda i, *_: (0, 0)),
                pl.BlockSpec((PEERS, ROWS + PAD, IDIM), lambda i, *_: (0, 0, 0)),
            ]
            + [pl.BlockSpec(p.shape, lambda i, *_: (0, 0)) for p in pieces],
            out_specs=(
                pl.BlockSpec((SHARE, TOTAL), lambda i, *_: (0, 0)),
                pl.BlockSpec((TOTAL, IDIM), lambda i, *_: (0, 0)),
                pl.BlockSpec((1, PEERS * ROWS, WIDE), lambda i, *_: (i, 0, 0)),
            ),
            scratch_shapes=[
                pltpu.VMEM((PEERS, ROWS, IDIM), jnp.float32),
                pltpu.VMEM((SHARE, TOTAL), jnp.float32),
            ],
        ),
        compiler_params=pltpu.CompilerParams(vmem_limit_bytes=60 * MIB),
        cost_estimate=pl.CostEstimate(
            flops=8 * PEERS * ROWS * TOTAL * IDIM, bytes_accessed=20 * MIB, transcendentals=0
        ),
        name="probs",
    )(ids, table, loss, qw, *pieces)


def coef_tile(coefs, g, gates_ref):
    g = jnp.broadcast_to(g[:, None, :], (SHARE, PEERS, WIDE)).reshape(ROWS, WIDE)
    for h in range(PEERS):
        part = slice(h * ROWS, (h + 1) * ROWS)
        coefs[part, :] = (g * gates_ref[0, part, :].astype(jnp.float32)).astype(jnp.bfloat16)


def kterm_tile(coefs, q_t):
    kterm = jnp.dot(q_t[...], coefs[...], preferred_element_type=jnp.float32)
    return (kterm * jnp.float32(ISCALE)).T


def grad_kernel(starts, ids, prob_ref, keys_ref, gates_ref, loss_ref, *refs):
    raws = refs[: len(starts)]
    qgrad_ref, kterm_ref, half_ref, q_t, grad, acc, coefs = refs[len(starts) :]
    qw_ref = raws[0]
    step = pl.program_id(0)

    @pl.when(step == 0)
    def _():
        mass = None
        done = 0
        for ref, start in zip(raws, starts):
            for place in range(start, ref.shape[1], SHARE):
                part = ref[0, place : place + SHARE, :].astype(jnp.float32)
                for p in range(1, PEERS):
                    part = part + ref[p, place : place + SHARE, :].astype(jnp.float32)
                col = (PLACE[done // 2] * 2 + done % 2) * IDIM
                grad[:, col : col + IDIM] = part
                mass = part if mass is None else mass + part
                done += 1
        mass = loss_ref[:, :1] / jnp.sum(mass, axis=1, keepdims=True)
        for b in range(BLOCKS):
            cols = slice(b * ROWS, (b + 1) * ROWS)
            grad[:, cols] = prob_ref[:, cols] - grad[:, cols] * mass
        half_ref[...] = grad[:, :HALF]
        for h in range(PEERS):
            q_t[:, h * ROWS : (h + 1) * ROWS] = qw_ref[h, :ROWS, :].T
        acc[...] = jnp.zeros_like(acc)

    rows = pl.ds(pl.multiple_of(step * WIDE, WIDE), WIDE)
    coef_tile(coefs, grad[:, rows], gates_ref)
    acc[...] += jnp.dot(coefs[...], keys_ref[rows, :], preferred_element_type=jnp.float32)
    for tile in range(HALF // WIDE, TOTAL // WIDE):

        @pl.when(step == tile)
        def _():
            kterm = kterm_tile(coefs, q_t)
            for i in range(WIDE // ROWS):
                place = ids[SORTED[tile * (WIDE // ROWS) + i]] >> 1
                place = pl.ds(pl.multiple_of(place * ROWS, ROWS), ROWS)
                kterm_ref[place, :] = kterm[i * ROWS : (i + 1) * ROWS, :]

    @pl.when(step == pl.num_programs(0) - 1)
    def _():
        for h in range(PEERS):
            qgrad = acc[h * ROWS : (h + 1) * ROWS, :] * jnp.float32(ISCALE)
            qgrad_ref[h] = qgrad.astype(jnp.bfloat16)


def whole(a):
    return pl.BlockSpec(a.shape, lambda i, *_: (0,) * len(a.shape))


GATES = pl.BlockSpec((1, PEERS * ROWS, WIDE), lambda i, *_: (i, 0, 0))


def grad_call(ids, prob, keys, gates, loss, raws, starts):
    out_shape = (
        jax.ShapeDtypeStruct((PEERS, ROWS, IDIM), jnp.bfloat16),
        jax.ShapeDtypeStruct((HALF, IDIM), jnp.float32),
        pltpu.HBM((SHARE, HALF), jnp.float32),
        pltpu.HBM((IDIM, PEERS * ROWS), jnp.bfloat16),
    )
    return pl.pallas_call(
        functools.partial(grad_kernel, starts),
        out_shape=out_shape,
        grid_spec=pltpu.PrefetchScalarGridSpec(
            num_scalar_prefetch=1,
            grid=(TOTAL // WIDE,),
            in_specs=[whole(prob), whole(keys), GATES, whole(loss)] + [whole(r) for r in raws],
            out_specs=tuple(whole(o) for o in out_shape),
            scratch_shapes=[
                pltpu.VMEM((SHARE, TOTAL), jnp.float32),
                pltpu.VMEM((PEERS * ROWS, IDIM), jnp.float32),
                pltpu.VMEM((PEERS * ROWS, WIDE), jnp.bfloat16),
            ],
        ),
        compiler_params=pltpu.CompilerParams(vmem_limit_bytes=50 * MIB),
        cost_estimate=pl.CostEstimate(
            flops=6 * PEERS * ROWS * TOTAL * IDIM, bytes_accessed=26 * MIB, transcendentals=0
        ),
        name="grads",
    )(ids, in_hbm(prob), in_hbm(keys), in_hbm(gates), loss, *raws)


def kterm_kernel(ids, half_ref, gates_ref, q_t, other_ref, out_ref, coefs):
    step = pl.program_id(0)
    for tile in range(HALF // WIDE):

        @pl.when(step == tile)
        def _():
            coef_tile(coefs, half_ref[:, tile * WIDE : (tile + 1) * WIDE], gates_ref)
            kterm = kterm_tile(coefs, q_t)
            for i in range(WIDE // ROWS):
                place = ids[SORTED[tile * (WIDE // ROWS) + i]] >> 1
                place = pl.ds(pl.multiple_of(place * ROWS, ROWS), ROWS)
                part = kterm[i * ROWS : (i + 1) * ROWS, :] + other_ref[place, :]
                out_ref[place, :] = part.astype(jnp.bfloat16)


def kterm_call(ids, half, gates, q_t, other):
    out = jax.ShapeDtypeStruct((HALF, IDIM), jnp.bfloat16)
    return pl.pallas_call(
        kterm_kernel,
        out_shape=out,
        grid_spec=pltpu.PrefetchScalarGridSpec(
            num_scalar_prefetch=1,
            grid=(HALF // WIDE,),
            in_specs=[whole(half), GATES, whole(q_t), whole(other)],
            out_specs=whole(out),
            scratch_shapes=[pltpu.VMEM((PEERS * ROWS, WIDE), jnp.bfloat16)],
        ),
        compiler_params=pltpu.CompilerParams(vmem_limit_bytes=50 * MIB),
        cost_estimate=pl.CostEstimate(
            flops=2 * PEERS * ROWS * TOTAL * IDIM, bytes_accessed=12 * MIB, transcendentals=0
        ),
        name="kterms",
    )(ids, in_hbm(half), in_hbm(gates), in_hbm(q_t), other)


def shift(array, axis, size, by):
    return lax.ppermute(array, axis, [(i, (i + by) % size) for i in range(size)])


def local(
    main_queries, latents, saved_lse, index_queries, index_keys, head_weights, row_weight,
    block_offsets,
):
    c0, c1, c2 = (lax.axis_index(a) for a in CTX)
    head = lax.axis_index(HEAD)
    ids = [(c0 ^ a) * 8 + ((c1 + b) & 3) * 2 + (c2 ^ c) for a, b, c in ORDER]
    ids = jnp.stack([i.astype(jnp.int32) for i in ids + [head]])

    own = jnp.concatenate([index_keys, latents], axis=1)
    core = functools.partial(shift, axis="ctx_2", size=2, by=1)
    up = functools.partial(shift, axis="ctx_1", size=4, by=1)
    down = functools.partial(shift, axis="ctx_1", size=4, by=-1)
    side = functools.partial(shift, axis="ctx_0", size=2, by=1)

    weights = head_weights.reshape(PEERS, 2, IDIM)
    weights = jnp.pad(weights, ((0, 0), (0, PAD - 2), (0, 0)))
    qw = jnp.concatenate([index_queries.reshape(PEERS, ROWS, IDIM), weights], axis=1)

    q_t = jnp.transpose(main_queries, (1, 2, 0))
    lse_t = saved_lse.T
    loss = lax.dynamic_slice_in_dim(row_weight, head * SHARE, SHARE, 0)
    loss = jnp.broadcast_to(loss[:, None], (SHARE, IDIM))
    q_t, lse_t, loss, qw, ids = lax.optimization_barrier((q_t, lse_t, loss, qw, ids))
    mass = functools.partial(mass_call, ids, block_offsets, q_t, lse_t)

    q_t = jnp.transpose(main_queries, (1, 2, 0))
    lse_t = saved_lse.T
    loss = lax.dynamic_slice_in_dim(row_weight, head * SHARE, SHARE, 0)
    loss = jnp.broadcast_to(loss[:, None], (SHARE, IDIM))
    q_t, lse_t, loss, qw, ids = lax.optimization_barrier((q_t, lse_t, loss, qw, ids))
    mass = functools.partial(mass_call, ids, block_offsets, q_t, lse_t)

    pair = core(own)
    z, yp, ym = side(own), up(own), down(own)
    near, keys_0 = mass([own, pair], 0)
    z, yp, ym, near = lax.optimization_barrier((z, yp, ym, near))
    zyp, zym, y2 = up(z), down(z), up(yp)
    pz, pyp, pym = core(z), core(yp), core(ym)
    raw_0, keys_1 = mass([z, yp, ym, pz, pyp, pym], 2, (qw, near))
    zyp, zym, raw_0 = lax.optimization_barrier((zyp, zym, raw_0))
    pzyp, pzym, py2 = core(zyp), core(zym), core(y2)
    zy2, pzy2 = down(zym), up(pzyp)
    raw_0 = lax.all_to_all(raw_0, HEAD, 0, 0, tiled=True)
    far, keys_2 = mass([zyp, zym, y2, pzyp, pzym, py2], 8)
    raw_1, keys_3 = mass([zy2, pzy2], 14, (far,))
    raw_1 = lax.all_to_all(raw_1, HEAD, 0, 0, tiled=True)

    prob, keys, gates = prob_call(ids, block_offsets, loss, raw_0, (keys_0, keys_1, keys_2, keys_3))
    qgrad, other, half, i_t = grad_call(
        ids, prob, keys, gates, loss, (raw_0, raw_1), (ROWS + PAD, 0)
    )
    other = core(other)
    qgrad = lax.all_to_all(qgrad, HEAD, 0, 0, tiled=True)
    kterm = kterm_call(ids, half, gates, i_t, other)
    kterm = kterm.reshape(HALF // SHARE, SHARE, IDIM)
    kterm = lax.all_to_all(kterm, CTX[:2] + HEAD, 0, 0, tiled=True)
    query_grads = qgrad.reshape(ROWS, PEERS, IDIM).astype(jnp.float32)
    key_grads = jnp.sum(kterm.astype(jnp.float32), axis=0)
    return query_grads, key_grads


def solution(mesh):
    torus = Mesh(mesh.devices.reshape(2, 4, 2, 4, 2), ALL)
    placed = (
        P(CTX, HEAD, None), P(CTX, None), P(CTX, HEAD), P(CTX, HEAD, None), P(CTX, None),
        P(CTX, HEAD), P(CTX), P(),
    )
    return jax.shard_map(
        local,
        mesh=torus,
        in_specs=placed,
        out_specs=(P(CTX, HEAD, None), P(ALL, None)),
        check_vma=False,
    )
```

```python
import functools

import jax
import jax.numpy as jnp
from jax import lax
from jax.experimental import pallas as pl
from jax.experimental.pallas import tpu as pltpu
from jax.sharding import Mesh
from jax.sharding import PartitionSpec as P

CTX = ("ctx_0", "ctx_1", "ctx_2")
HEAD = ("head_0", "head_1")
ALL = CTX + HEAD

ROWS = 256
LATENT = 576
IDIM = 128
HEADS_DEV = 16
PEERS = 8
SHARE = ROWS // PEERS
BLOCKS = 16
TOTAL = BLOCKS * ROWS
PAD = 16
LOG2E = 1.4426950408889634
SCORE = 192.0 ** -0.5
ISCALE = IDIM ** -0.5
WIDE = 1024
MIB = 2**20

ORDER = (
    (0, 0, 0), (0, 0, 1),
    (1, 0, 0), (0, 3, 0), (0, 1, 0), (1, 0, 1), (0, 3, 1), (0, 1, 1),
    (1, 3, 0), (1, 1, 0), (0, 2, 0), (1, 3, 1), (1, 1, 1), (0, 2, 1), (1, 2, 0), (1, 2, 1),
)

SORTED = tuple(k for p in range(2) for k in range(BLOCKS) if ORDER[k][2] == p)
PLACE = tuple(SORTED.index(k) for k in range(BLOCKS))
HALF = TOTAL // 2
VMEM = pltpu.VMEM


def in_hbm(array):
    return pltpu.with_memory_space_constraint(array, pltpu.HBM)


def mass_kernel(first, count, carried, hstep, ids, table, q_ref, lse_ref, *refs):
    blocks, extra = refs[:count], refs[count : count + carried]
    out_ref, keys_ref, acc = refs[count + carried :]
    step = pl.program_id(0)

    @pl.when(step == 0)
    def _():
        acc[...] = jnp.zeros_like(acc)
        for b in range(count):
            keys_ref[b * ROWS : (b + 1) * ROWS, :] = blocks[b][:, :IDIM]

    for b in range(count):
        lat = blocks[b][:, IDIM : IDIM + LATENT]
        rows = slice(b * ROWS, (b + 1) * ROWS)
        part = None
        for i in range(hstep):
            s = jnp.dot(lat, q_ref[step * hstep + i], preferred_element_type=jnp.float32)
            lse = lse_ref[pl.ds(step * hstep + i, 1), :] * jnp.float32(LOG2E)
            e = jnp.exp2(s * jnp.float32(SCORE * LOG2E) - lse)
            part = e if part is None else part + e
        acc[rows, :] += part

    @pl.when(step == pl.num_programs(0) - 1)
    def _():
        place = 0
        for ref in extra:
            size = ref.shape[1]
            out_ref[:, place : place + size, :] = ref[...]
            place += size
        q_pos = table[ids[0]] + lax.broadcasted_iota(jnp.int32, (ROWS, ROWS), 0)
        for b in range(count):
            k_pos = table[ids[first + b]] + lax.broadcasted_iota(jnp.int32, (ROWS, ROWS), 1)
            mass = acc[b * ROWS : (b + 1) * ROWS, :].T
            mass = jnp.where(k_pos <= q_pos, mass, jnp.float32(0.0)).astype(jnp.bfloat16)
            for i in range(2):
                half = mass[:, i * IDIM : (i + 1) * IDIM].reshape(PEERS, SHARE, IDIM)
                out_ref[:, place : place + SHARE, :] = half
                place += SHARE


def mass_call(ids, table, q_t, lse_t, blocks, first, extra=(), hstep=HEADS_DEV):
    count = len(blocks)
    width = blocks[0].shape[1]
    rows = sum(e.shape[1] for e in extra) + count * 2 * SHARE
    return pl.pallas_call(
        functools.partial(mass_kernel, first, count, len(extra), hstep),
        out_shape=(
            jax.ShapeDtypeStruct((PEERS, rows, IDIM), jnp.bfloat16),
            pltpu.HBM((count * ROWS, IDIM), jnp.bfloat16),
        ),
        grid_spec=pltpu.PrefetchScalarGridSpec(
            num_scalar_prefetch=2,
            grid=(HEADS_DEV // hstep,),
            in_specs=[
                pl.BlockSpec(memory_space=VMEM),
                pl.BlockSpec((HEADS_DEV, ROWS), lambda h, *_: (0, 0)),
            ]
            + [pl.BlockSpec((ROWS, width), lambda h, *_: (0, 0))] * count
            + [pl.BlockSpec(e.shape, lambda h, *_: (0, 0, 0)) for e in extra],
            out_specs=(
                pl.BlockSpec((PEERS, rows, IDIM), lambda h, *_: (0, 0, 0)),
                pl.BlockSpec((count * ROWS, IDIM), lambda h, *_: (0, 0)),
            ),
            scratch_shapes=[pltpu.VMEM((count * ROWS, ROWS), jnp.float32)],
        ),
        compiler_params=pltpu.CompilerParams(vmem_limit_bytes=28 * MIB),
        cost_estimate=pl.CostEstimate(
            flops=2 * HEADS_DEV * ROWS * ROWS * count * LATENT * 4 // 3,
            bytes_accessed=HEADS_DEV * ROWS * LATENT * 2 + count * ROWS * (width + ROWS) * 2,
            transcendentals=HEADS_DEV * ROWS * ROWS * count,
        ),
        name="mass_%d" % first,
    )(ids, table, q_t, lse_t, *blocks, *extra)


def loss_rows(ids, loss_ref, turned):
    first = ids[BLOCKS] * SHARE
    row = loss_ref[pl.ds(first // IDIM, 1), :]
    turned[...] = jnp.broadcast_to(row, (IDIM, IDIM)).T
    return turned[pl.ds(pl.multiple_of(first % IDIM, SHARE), SHARE), :1]


def prob_kernel(ids, table, loss_ref, qw_ref, *refs):
    pieces = refs[:-6]
    prob_ref, keys_ref, gates_ref, wide, logit, turned = refs[-6:]
    step = pl.program_id(0)

    @pl.when(step == 0)
    def _():
        done = 0
        for piece in pieces:
            for start in range(0, piece.shape[0], ROWS):
                place = PLACE[done] * ROWS
                keys_ref[place : place + ROWS, :] = piece[start : start + ROWS, :]
                done += 1
        for h in range(PEERS):
            w = qw_ref[h, ROWS : ROWS + PAD, :].astype(jnp.float32)
            for i in range(2):
                wide[h, i * IDIM : (i + 1) * IDIM, :] = jnp.broadcast_to(
                    w[i : i + 1, :], (IDIM, IDIM)
                ).T

    count = WIDE // IDIM
    start = pl.multiple_of(step * WIDE, WIDE)
    keys = keys_ref[pl.ds(start, WIDE), :]
    acc = [None] * count
    for h in range(PEERS):
        dots = lax.dot_general(
            qw_ref[h, :ROWS, :], keys, (((1,), (1,)), ((), ())),
            preferred_element_type=jnp.float32,
        )
        w = wide[h]
        rows = slice(h * ROWS, (h + 1) * ROWS)
        for i in range(count):
            cols = slice(i * IDIM, (i + 1) * IDIM)
            gate = jnp.where(dots[:, cols] > 0, w, jnp.float32(0.0))
            gates_ref[0, rows, cols] = gate.astype(jnp.bfloat16)
            y = gate * dots[:, cols]
            acc[i] = y if acc[i] is None else acc[i] + y
    for i in range(count):
        cols = pl.ds(pl.multiple_of(start + i * IDIM, IDIM), IDIM)
        logit[:, cols] = jnp.sum(acc[i].reshape(SHARE, PEERS, IDIM), axis=1)

    @pl.when(step == pl.num_programs(0) - 1)
    def _():
        sub = ids[BLOCKS] * SHARE
        q_pos = table[ids[0]] + sub + lax.broadcasted_iota(jnp.int32, (SHARE, ROWS), 0)
        lane = lax.broadcasted_iota(jnp.int32, (SHARE, ROWS), 1)
        peak = None
        for b in range(BLOCKS):
            cols = slice(b * ROWS, (b + 1) * ROWS)
            masked = jnp.where(
                table[ids[SORTED[b]]] + lane <= q_pos,
                logit[:, cols] * jnp.float32(ISCALE),
                jnp.float32(-1e30),
            )
            logit[:, cols] = masked
            peak = masked if peak is None else jnp.maximum(peak, masked)
        peak = jnp.max(peak, axis=1, keepdims=True)
        total = None
        for b in range(BLOCKS):
            cols = slice(b * ROWS, (b + 1) * ROWS)
            e = jnp.exp(logit[:, cols] - peak)
            logit[:, cols] = e
            total = e if total is None else total + e
        total = loss_rows(ids, loss_ref, turned) / jnp.sum(total, axis=1, keepdims=True)
        for b in range(BLOCKS):
            cols = slice(b * ROWS, (b + 1) * ROWS)
            prob_ref[:, cols] = logit[:, cols] * total


def prob_call(ids, table, loss, qw, pieces):
    return pl.pallas_call(
        prob_kernel,
        out_shape=(
            jax.ShapeDtypeStruct((SHARE, TOTAL), jnp.float32),
            jax.ShapeDtypeStruct((TOTAL, IDIM), jnp.bfloat16),
            jax.ShapeDtypeStruct((TOTAL // WIDE, PEERS * ROWS, WIDE), jnp.bfloat16),
        ),
        grid_spec=pltpu.PrefetchScalarGridSpec(
            num_scalar_prefetch=2,
            grid=(TOTAL // WIDE,),
            in_specs=[
                pl.BlockSpec(loss.shape, lambda i, *_: (0, 0)),
                pl.BlockSpec((PEERS, ROWS + PAD, IDIM), lambda i, *_: (0, 0, 0)),
            ]
            + [pl.BlockSpec(p.shape, lambda i, *_: (0, 0)) for p in pieces],
            out_specs=(
                pl.BlockSpec((SHARE, TOTAL), lambda i, *_: (0, 0)),
                pl.BlockSpec((TOTAL, IDIM), lambda i, *_: (0, 0)),
                pl.BlockSpec((1, PEERS * ROWS, WIDE), lambda i, *_: (i, 0, 0)),
            ),
            scratch_shapes=[
                pltpu.VMEM((PEERS, ROWS, IDIM), jnp.float32),
                pltpu.VMEM((SHARE, TOTAL), jnp.float32),
                pltpu.VMEM((IDIM, IDIM), jnp.float32),
            ],
        ),
        compiler_params=pltpu.CompilerParams(vmem_limit_bytes=60 * MIB),
        cost_estimate=pl.CostEstimate(
            flops=8 * PEERS * ROWS * TOTAL * IDIM, bytes_accessed=20 * MIB, transcendentals=0
        ),
        name="probs",
    )(ids, table, loss, qw, *pieces)


def coef_tile(coefs, g, gates_ref):
    g = jnp.broadcast_to(g[:, None, :], (SHARE, PEERS, WIDE)).reshape(ROWS, WIDE)
    for h in range(PEERS):
        part = slice(h * ROWS, (h + 1) * ROWS)
        coefs[part, :] = (g * gates_ref[0, part, :].astype(jnp.float32)).astype(jnp.bfloat16)


def kterm_tile(coefs, q_t):
    kterm = jnp.dot(q_t[...], coefs[...], preferred_element_type=jnp.float32)
    return (kterm * jnp.float32(ISCALE)).T


def grad_kernel(starts, ids, prob_ref, keys_ref, gates_ref, loss_ref, *refs):
    raws = refs[: len(starts)]
    qgrad_ref, kterm_ref, half_ref, q_t, grad, acc, coefs, turned = refs[len(starts) :]
    qw_ref = raws[0]
    step = pl.program_id(0)

    @pl.when(step == 0)
    def _():
        mass = None
        done = 0
        for ref, start in zip(raws, starts):
            for place in range(start, ref.shape[1], SHARE):
                part = ref[0, place : place + SHARE, :].astype(jnp.float32)
                for p in range(1, PEERS):
                    part = part + ref[p, place : place + SHARE, :].astype(jnp.float32)
                col = (PLACE[done // 2] * 2 + done % 2) * IDIM
                grad[:, col : col + IDIM] = part
                mass = part if mass is None else mass + part
                done += 1
        mass = loss_rows(ids, loss_ref, turned) / jnp.sum(mass, axis=1, keepdims=True)
        for b in range(BLOCKS):
            cols = slice(b * ROWS, (b + 1) * ROWS)
            grad[:, cols] = prob_ref[:, cols] - grad[:, cols] * mass
        half_ref[...] = grad[:, :HALF]
        for h in range(PEERS):
            q_t[:, h * ROWS : (h + 1) * ROWS] = qw_ref[h, :ROWS, :].T
        acc[...] = jnp.zeros_like(acc)

    rows = pl.ds(pl.multiple_of(step * WIDE, WIDE), WIDE)
    coef_tile(coefs, grad[:, rows], gates_ref)
    acc[...] += jnp.dot(coefs[...], keys_ref[rows, :], preferred_element_type=jnp.float32)
    for tile in range(HALF // WIDE, TOTAL // WIDE):

        @pl.when(step == tile)
        def _():
            kterm = kterm_tile(coefs, q_t)
            for i in range(WIDE // ROWS):
                place = ids[SORTED[tile * (WIDE // ROWS) + i]] >> 1
                place = pl.ds(pl.multiple_of(place * ROWS, ROWS), ROWS)
                kterm_ref[place, :] = kterm[i * ROWS : (i + 1) * ROWS, :]

    @pl.when(step == pl.num_programs(0) - 1)
    def _():
        for h in range(PEERS):
            qgrad = acc[h * ROWS : (h + 1) * ROWS, :] * jnp.float32(ISCALE)
            qgrad_ref[h] = qgrad.astype(jnp.bfloat16)


def whole(a):
    return pl.BlockSpec(a.shape, lambda i, *_: (0,) * len(a.shape))


GATES = pl.BlockSpec((1, PEERS * ROWS, WIDE), lambda i, *_: (i, 0, 0))


def grad_call(ids, prob, keys, gates, loss, raws, starts):
    out_shape = (
        jax.ShapeDtypeStruct((PEERS, ROWS, IDIM), jnp.bfloat16),
        jax.ShapeDtypeStruct((HALF, IDIM), jnp.float32),
        pltpu.HBM((SHARE, HALF), jnp.float32),
        pltpu.HBM((IDIM, PEERS * ROWS), jnp.bfloat16),
    )
    return pl.pallas_call(
        functools.partial(grad_kernel, starts),
        out_shape=out_shape,
        grid_spec=pltpu.PrefetchScalarGridSpec(
            num_scalar_prefetch=1,
            grid=(TOTAL // WIDE,),
            in_specs=[whole(prob), whole(keys), GATES, whole(loss)] + [whole(r) for r in raws],
            out_specs=tuple(whole(o) for o in out_shape),
            scratch_shapes=[
                pltpu.VMEM((SHARE, TOTAL), jnp.float32),
                pltpu.VMEM((PEERS * ROWS, IDIM), jnp.float32),
                pltpu.VMEM((PEERS * ROWS, WIDE), jnp.bfloat16),
                pltpu.VMEM((IDIM, IDIM), jnp.float32),
            ],
        ),
        compiler_params=pltpu.CompilerParams(vmem_limit_bytes=50 * MIB),
        cost_estimate=pl.CostEstimate(
            flops=6 * PEERS * ROWS * TOTAL * IDIM, bytes_accessed=26 * MIB, transcendentals=0
        ),
        name="grads",
    )(ids, in_hbm(prob), in_hbm(keys), in_hbm(gates), loss, *raws)


def kterm_kernel(ids, half_ref, gates_ref, q_t, other_ref, out_ref, coefs):
    step = pl.program_id(0)
    for tile in range(HALF // WIDE):

        @pl.when(step == tile)
        def _():
            coef_tile(coefs, half_ref[:, tile * WIDE : (tile + 1) * WIDE], gates_ref)
            kterm = kterm_tile(coefs, q_t)
            for i in range(WIDE // ROWS):
                place = ids[SORTED[tile * (WIDE // ROWS) + i]] >> 1
                place = pl.ds(pl.multiple_of(place * ROWS, ROWS), ROWS)
                part = kterm[i * ROWS : (i + 1) * ROWS, :] + other_ref[place, :]
                out_ref[place, :] = part.astype(jnp.bfloat16)


def kterm_call(ids, half, gates, q_t, other):
    out = jax.ShapeDtypeStruct((HALF, IDIM), jnp.bfloat16)
    return pl.pallas_call(
        kterm_kernel,
        out_shape=out,
        grid_spec=pltpu.PrefetchScalarGridSpec(
            num_scalar_prefetch=1,
            grid=(HALF // WIDE,),
            in_specs=[whole(half), GATES, whole(q_t), whole(other)],
            out_specs=whole(out),
            scratch_shapes=[pltpu.VMEM((PEERS * ROWS, WIDE), jnp.bfloat16)],
        ),
        compiler_params=pltpu.CompilerParams(vmem_limit_bytes=50 * MIB),
        cost_estimate=pl.CostEstimate(
            flops=2 * PEERS * ROWS * TOTAL * IDIM, bytes_accessed=12 * MIB, transcendentals=0
        ),
        name="kterms",
    )(ids, in_hbm(half), in_hbm(gates), in_hbm(q_t), other)


def shift(array, axis, size, by):
    return lax.ppermute(array, axis, [(i, (i + by) % size) for i in range(size)])


def local(
    main_queries, latents, saved_lse, index_queries, index_keys, head_weights, row_weight,
    block_offsets,
):
    c0, c1, c2 = (lax.axis_index(a) for a in CTX)
    head = lax.axis_index(HEAD)
    ids = [(c0 ^ a) * 8 + ((c1 + b) & 3) * 2 + (c2 ^ c) for a, b, c in ORDER]
    ids = jnp.stack([i.astype(jnp.int32) for i in ids + [head]])

    own = jnp.concatenate([index_keys, latents], axis=1)
    core = functools.partial(shift, axis="ctx_2", size=2, by=1)
    up = functools.partial(shift, axis="ctx_1", size=4, by=1)
    down = functools.partial(shift, axis="ctx_1", size=4, by=-1)
    side = functools.partial(shift, axis="ctx_0", size=2, by=1)

    weights = head_weights.reshape(PEERS, 2, IDIM)
    weights = jnp.pad(weights, ((0, 0), (0, PAD - 2), (0, 0)))
    qw = jnp.concatenate([index_queries.reshape(PEERS, ROWS, IDIM), weights], axis=1)

    q_t = jnp.transpose(main_queries, (1, 2, 0))
    lse_t = saved_lse.T
    loss = row_weight.reshape(ROWS // IDIM, IDIM)
    q_t, lse_t, loss, qw, ids = lax.optimization_barrier((q_t, lse_t, loss, qw, ids))
    mass = functools.partial(mass_call, ids, block_offsets, q_t, lse_t)

    q_t = jnp.transpose(main_queries, (1, 2, 0))
    lse_t = saved_lse.T
    loss = row_weight.reshape(ROWS // IDIM, IDIM)
    q_t, lse_t, loss, qw, ids = lax.optimization_barrier((q_t, lse_t, loss, qw, ids))
    mass = functools.partial(mass_call, ids, block_offsets, q_t, lse_t)

    pair = core(own)
    z, yp, ym = side(own), up(own), down(own)
    near, keys_0 = mass([own, pair], 0)
    z, yp, ym, near = lax.optimization_barrier((z, yp, ym, near))
    zyp, zym, y2 = up(z), down(z), up(yp)
    pz, pyp, pym = core(z), core(yp), core(ym)
    raw_0, keys_1 = mass([z, yp, ym, pz, pyp, pym], 2, (qw, near))
    zyp, zym, raw_0 = lax.optimization_barrier((zyp, zym, raw_0))
    pzyp, pzym, py2 = core(zyp), core(zym), core(y2)
    zy2, pzy2 = down(zym), up(pzyp)
    raw_0 = lax.all_to_all(raw_0, HEAD, 0, 0, tiled=True)
    far, keys_2 = mass([zyp, zym, y2, pzyp, pzym, py2], 8)
    raw_1, keys_3 = mass([zy2, pzy2], 14, (far,))
    raw_1 = lax.all_to_all(raw_1, HEAD, 0, 0, tiled=True)

    prob, keys, gates = prob_call(ids, block_offsets, loss, raw_0, (keys_0, keys_1, keys_2, keys_3))
    qgrad, other, half, i_t = grad_call(
        ids, prob, keys, gates, loss, (raw_0, raw_1), (ROWS + PAD, 0)
    )
    other = core(other)
    qgrad = lax.all_to_all(qgrad, HEAD, 0, 0, tiled=True)
    kterm = kterm_call(ids, half, gates, i_t, other)
    kterm = kterm.reshape(HALF // SHARE, SHARE, IDIM)
    kterm = lax.all_to_all(kterm, CTX[:2] + HEAD, 0, 0, tiled=True)
    query_grads = qgrad.reshape(ROWS, PEERS, IDIM).astype(jnp.float32)
    key_grads = jnp.sum(kterm.astype(jnp.float32), axis=0)
    return query_grads, key_grads


def solution(mesh):
    torus = Mesh(mesh.devices.reshape(2, 4, 2, 4, 2), ALL)
    placed = (
        P(CTX, HEAD, None), P(CTX, None), P(CTX, HEAD), P(CTX, HEAD, None), P(CTX, None),
        P(CTX, HEAD), P(CTX), P(),
    )
    return jax.shard_map(
        local,
        mesh=torus,
        in_specs=placed,
        out_specs=(P(CTX, HEAD, None), P(ALL, None)),
        check_vma=False,
    )
```

```python
import functools

import jax
import jax.numpy as jnp
from jax import lax
from jax.experimental import pallas as pl
from jax.experimental.pallas import tpu as pltpu
from jax.sharding import Mesh
from jax.sharding import PartitionSpec as P

CTX = ("ctx_0", "ctx_1", "ctx_2")
HEAD = ("head_0", "head_1")
ALL = CTX + HEAD

ROWS = 256
LATENT = 576
IDIM = 128
HEADS_DEV = 16
PEERS = 8
SHARE = ROWS // PEERS
BLOCKS = 16
TOTAL = BLOCKS * ROWS
PAD = 16
LOG2E = 1.4426950408889634
SCORE = 192.0 ** -0.5
ISCALE = IDIM ** -0.5
WIDE = 1024
MIB = 2**20

ORDER = (
    (0, 0, 0), (0, 0, 1),
    (1, 0, 0), (0, 3, 0), (0, 1, 0), (1, 0, 1), (0, 3, 1), (0, 1, 1),
    (1, 3, 0), (1, 1, 0), (0, 2, 0), (1, 3, 1), (1, 1, 1), (0, 2, 1), (1, 2, 0), (1, 2, 1),
)

SORTED = tuple(k for p in range(2) for k in range(BLOCKS) if ORDER[k][2] == p)
PLACE = tuple(SORTED.index(k) for k in range(BLOCKS))
HALF = TOTAL // 2
VMEM = pltpu.VMEM


def in_hbm(array):
    return pltpu.with_memory_space_constraint(array, pltpu.HBM)


def mass_kernel(first, count, carried, hstep, ids, table, q_ref, lse_ref, *refs):
    blocks, extra = refs[:count], refs[count : count + carried]
    out_ref, keys_ref, acc = refs[count + carried :]
    step = pl.program_id(0)

    @pl.when(step == 0)
    def _():
        acc[...] = jnp.zeros_like(acc)
        for b in range(count):
            keys_ref[b * ROWS : (b + 1) * ROWS, :] = blocks[b][:, :IDIM]

    for b in range(count):
        lat = blocks[b][:, IDIM : IDIM + LATENT]
        rows = slice(b * ROWS, (b + 1) * ROWS)
        part = None
        for i in range(hstep):
            s = jnp.dot(lat, q_ref[step * hstep + i], preferred_element_type=jnp.float32)
            lse = lse_ref[pl.ds(step * hstep + i, 1), :] * jnp.float32(LOG2E)
            e = jnp.exp2(s * jnp.float32(SCORE * LOG2E) - lse)
            part = e if part is None else part + e
        acc[rows, :] += part

    @pl.when(step == pl.num_programs(0) - 1)
    def _():
        place = 0
        for ref in extra:
            size = ref.shape[1]
            out_ref[:, place : place + size, :] = ref[...]
            place += size
        q_pos = table[ids[0]] + lax.broadcasted_iota(jnp.int32, (ROWS, ROWS), 0)
        for b in range(count):
            k_pos = table[ids[first + b]] + lax.broadcasted_iota(jnp.int32, (ROWS, ROWS), 1)
            mass = acc[b * ROWS : (b + 1) * ROWS, :].T
            mass = jnp.where(k_pos <= q_pos, mass, jnp.float32(0.0)).astype(jnp.bfloat16)
            for i in range(2):
                half = mass[:, i * IDIM : (i + 1) * IDIM].reshape(PEERS, SHARE, IDIM)
                out_ref[:, place : place + SHARE, :] = half
                place += SHARE


def mass_call(ids, table, q_t, lse_t, blocks, first, extra=(), hstep=HEADS_DEV):
    count = len(blocks)
    width = blocks[0].shape[1]
    rows = sum(e.shape[1] for e in extra) + count * 2 * SHARE
    return pl.pallas_call(
        functools.partial(mass_kernel, first, count, len(extra), hstep),
        out_shape=(
            jax.ShapeDtypeStruct((PEERS, rows, IDIM), jnp.bfloat16),
            pltpu.HBM((count * ROWS, IDIM), jnp.bfloat16),
        ),
        grid_spec=pltpu.PrefetchScalarGridSpec(
            num_scalar_prefetch=2,
            grid=(HEADS_DEV // hstep,),
            in_specs=[
                pl.BlockSpec(memory_space=VMEM),
                pl.BlockSpec((HEADS_DEV, ROWS), lambda h, *_: (0, 0)),
            ]
            + [pl.BlockSpec((ROWS, width), lambda h, *_: (0, 0))] * count
            + [pl.BlockSpec(e.shape, lambda h, *_: (0, 0, 0)) for e in extra],
            out_specs=(
                pl.BlockSpec((PEERS, rows, IDIM), lambda h, *_: (0, 0, 0)),
                pl.BlockSpec((count * ROWS, IDIM), lambda h, *_: (0, 0)),
            ),
            scratch_shapes=[pltpu.VMEM((count * ROWS, ROWS), jnp.float32)],
        ),
        compiler_params=pltpu.CompilerParams(vmem_limit_bytes=28 * MIB),
        cost_estimate=pl.CostEstimate(
            flops=2 * HEADS_DEV * ROWS * ROWS * count * LATENT * 4 // 3,
            bytes_accessed=HEADS_DEV * ROWS * LATENT * 2 + count * ROWS * (width + ROWS) * 2,
            transcendentals=HEADS_DEV * ROWS * ROWS * count,
        ),
        name="mass_%d" % first,
    )(ids, table, q_t, lse_t, *blocks, *extra)


def loss_rows(ids, loss_ref, turned):
    first = ids[BLOCKS] * SHARE
    row = loss_ref[pl.ds(first // IDIM, 1), :]
    turned[...] = jnp.broadcast_to(row, (IDIM, IDIM)).T
    return turned[pl.ds(pl.multiple_of(first % IDIM, SHARE), SHARE), :1]


def prob_kernel(ids, table, loss_ref, qw_ref, *refs):
    pieces = refs[:-6]
    prob_ref, keys_ref, gates_ref, wide, logit, turned = refs[-6:]
    step = pl.program_id(0)

    @pl.when(step == 0)
    def _():
        done = 0
        for piece in pieces:
            for start in range(0, piece.shape[0], ROWS):
                place = PLACE[done] * ROWS
                keys_ref[place : place + ROWS, :] = piece[start : start + ROWS, :]
                done += 1
        for h in range(PEERS):
            w = qw_ref[h, ROWS : ROWS + PAD, :].astype(jnp.float32)
            for i in range(2):
                wide[h, i * IDIM : (i + 1) * IDIM, :] = jnp.broadcast_to(
                    w[i : i + 1, :], (IDIM, IDIM)
                ).T

    count = WIDE // IDIM
    start = pl.multiple_of(step * WIDE, WIDE)
    keys = keys_ref[pl.ds(start, WIDE), :]
    acc = [None] * count
    for h in range(PEERS):
        dots = lax.dot_general(
            qw_ref[h, :ROWS, :], keys, (((1,), (1,)), ((), ())),
            preferred_element_type=jnp.float32,
        )
        w = wide[h]
        rows = slice(h * ROWS, (h + 1) * ROWS)
        for i in range(count):
            cols = slice(i * IDIM, (i + 1) * IDIM)
            gate = jnp.where(dots[:, cols] > 0, w, jnp.float32(0.0))
            gates_ref[0, rows, cols] = gate.astype(jnp.bfloat16)
            y = gate * dots[:, cols]
            acc[i] = y if acc[i] is None else acc[i] + y
    for i in range(count):
        cols = pl.ds(pl.multiple_of(start + i * IDIM, IDIM), IDIM)
        logit[:, cols] = jnp.sum(acc[i].reshape(SHARE, PEERS, IDIM), axis=1)

    @pl.when(step == pl.num_programs(0) - 1)
    def _():
        sub = ids[BLOCKS] * SHARE
        q_pos = table[ids[0]] + sub + lax.broadcasted_iota(jnp.int32, (SHARE, ROWS), 0)
        lane = lax.broadcasted_iota(jnp.int32, (SHARE, ROWS), 1)
        peak = None
        for b in range(BLOCKS):
            cols = slice(b * ROWS, (b + 1) * ROWS)
            masked = jnp.where(
                table[ids[SORTED[b]]] + lane <= q_pos,
                logit[:, cols] * jnp.float32(ISCALE),
                jnp.float32(-1e30),
            )
            logit[:, cols] = masked
            peak = masked if peak is None else jnp.maximum(peak, masked)
        peak = jnp.max(peak, axis=1, keepdims=True)
        total = None
        for b in range(BLOCKS):
            cols = slice(b * ROWS, (b + 1) * ROWS)
            e = jnp.exp(logit[:, cols] - peak)
            logit[:, cols] = e
            total = e if total is None else total + e
        total = loss_rows(ids, loss_ref, turned) / jnp.sum(total, axis=1, keepdims=True)
        for b in range(BLOCKS):
            cols = slice(b * ROWS, (b + 1) * ROWS)
            prob_ref[:, cols] = logit[:, cols] * total


def prob_call(ids, table, loss, qw, pieces):
    return pl.pallas_call(
        prob_kernel,
        out_shape=(
            jax.ShapeDtypeStruct((SHARE, TOTAL), jnp.float32),
            jax.ShapeDtypeStruct((TOTAL, IDIM), jnp.bfloat16),
            jax.ShapeDtypeStruct((TOTAL // WIDE, PEERS * ROWS, WIDE), jnp.bfloat16),
        ),
        grid_spec=pltpu.PrefetchScalarGridSpec(
            num_scalar_prefetch=2,
            grid=(TOTAL // WIDE,),
            in_specs=[
                pl.BlockSpec(loss.shape, lambda i, *_: (0, 0)),
                pl.BlockSpec((PEERS, ROWS + PAD, IDIM), lambda i, *_: (0, 0, 0)),
            ]
            + [pl.BlockSpec(p.shape, lambda i, *_: (0, 0)) for p in pieces],
            out_specs=(
                pl.BlockSpec((SHARE, TOTAL), lambda i, *_: (0, 0)),
                pl.BlockSpec((TOTAL, IDIM), lambda i, *_: (0, 0)),
                pl.BlockSpec((1, PEERS * ROWS, WIDE), lambda i, *_: (i, 0, 0)),
            ),
            scratch_shapes=[
                pltpu.VMEM((PEERS, ROWS, IDIM), jnp.float32),
                pltpu.VMEM((SHARE, TOTAL), jnp.float32),
                pltpu.VMEM((IDIM, IDIM), jnp.float32),
            ],
        ),
        compiler_params=pltpu.CompilerParams(vmem_limit_bytes=60 * MIB),
        cost_estimate=pl.CostEstimate(
            flops=8 * PEERS * ROWS * TOTAL * IDIM, bytes_accessed=20 * MIB, transcendentals=0
        ),
        name="probs",
    )(ids, table, loss, qw, *pieces)


def coef_tile(coefs, g, gates_ref):
    g = jnp.broadcast_to(g[:, None, :], (SHARE, PEERS, WIDE)).reshape(ROWS, WIDE)
    for h in range(PEERS):
        part = slice(h * ROWS, (h + 1) * ROWS)
        coefs[part, :] = (g * gates_ref[0, part, :].astype(jnp.float32)).astype(jnp.bfloat16)


def kterm_tile(coefs, q_t):
    kterm = jnp.dot(q_t[...], coefs[...], preferred_element_type=jnp.float32)
    return (kterm * jnp.float32(ISCALE)).T


def grad_kernel(starts, ids, prob_ref, keys_ref, gates_ref, loss_ref, *refs):
    raws = refs[: len(starts)]
    qgrad_ref, kterm_ref, half_ref, q_t, grad, acc, coefs, turned = refs[len(starts) :]
    qw_ref = raws[0]
    step = pl.program_id(0)

    @pl.when(step == 0)
    def _():
        mass = None
        done = 0
        for ref, start in zip(raws, starts):
            for place in range(start, ref.shape[1], SHARE):
                part = ref[0, place : place + SHARE, :].astype(jnp.float32)
                for p in range(1, PEERS):
                    part = part + ref[p, place : place + SHARE, :].astype(jnp.float32)
                col = (PLACE[done // 2] * 2 + done % 2) * IDIM
                grad[:, col : col + IDIM] = part
                mass = part if mass is None else mass + part
                done += 1
        mass = loss_rows(ids, loss_ref, turned) / jnp.sum(mass, axis=1, keepdims=True)
        for b in range(BLOCKS):
            cols = slice(b * ROWS, (b + 1) * ROWS)
            grad[:, cols] = prob_ref[:, cols] - grad[:, cols] * mass
        half_ref[...] = grad[:, :HALF]
        for h in range(PEERS):
            q_t[:, h * ROWS : (h + 1) * ROWS] = qw_ref[h, :ROWS, :].T
        acc[...] = jnp.zeros_like(acc)

    rows = pl.ds(pl.multiple_of(step * WIDE, WIDE), WIDE)
    coef_tile(coefs, grad[:, rows], gates_ref)
    acc[...] += jnp.dot(coefs[...], keys_ref[rows, :], preferred_element_type=jnp.float32)
    for tile in range(HALF // WIDE, TOTAL // WIDE):

        @pl.when(step == tile)
        def _():
            kterm = kterm_tile(coefs, q_t)
            for i in range(WIDE // ROWS):
                place = ids[SORTED[tile * (WIDE // ROWS) + i]] >> 1
                place = pl.ds(pl.multiple_of(place * ROWS, ROWS), ROWS)
                kterm_ref[place, :] = kterm[i * ROWS : (i + 1) * ROWS, :]

    @pl.when(step == pl.num_programs(0) - 1)
    def _():
        for h in range(PEERS):
            qgrad = acc[h * ROWS : (h + 1) * ROWS, :] * jnp.float32(ISCALE)
            qgrad_ref[h] = qgrad.astype(jnp.bfloat16)


def whole(a):
    return pl.BlockSpec(a.shape, lambda i, *_: (0,) * len(a.shape))


GATES = pl.BlockSpec((1, PEERS * ROWS, WIDE), lambda i, *_: (i, 0, 0))


def grad_call(ids, prob, keys, gates, loss, raws, starts):
    out_shape = (
        jax.ShapeDtypeStruct((PEERS, ROWS, IDIM), jnp.bfloat16),
        jax.ShapeDtypeStruct((HALF, IDIM), jnp.float32),
        pltpu.HBM((SHARE, HALF), jnp.float32),
        pltpu.HBM((IDIM, PEERS * ROWS), jnp.bfloat16),
    )
    return pl.pallas_call(
        functools.partial(grad_kernel, starts),
        out_shape=out_shape,
        grid_spec=pltpu.PrefetchScalarGridSpec(
            num_scalar_prefetch=1,
            grid=(TOTAL // WIDE,),
            in_specs=[whole(prob), whole(keys), GATES, whole(loss)] + [whole(r) for r in raws],
            out_specs=tuple(whole(o) for o in out_shape),
            scratch_shapes=[
                pltpu.VMEM((SHARE, TOTAL), jnp.float32),
                pltpu.VMEM((PEERS * ROWS, IDIM), jnp.float32),
                pltpu.VMEM((PEERS * ROWS, WIDE), jnp.bfloat16),
                pltpu.VMEM((IDIM, IDIM), jnp.float32),
            ],
        ),
        compiler_params=pltpu.CompilerParams(vmem_limit_bytes=50 * MIB),
        cost_estimate=pl.CostEstimate(
            flops=6 * PEERS * ROWS * TOTAL * IDIM, bytes_accessed=26 * MIB, transcendentals=0
        ),
        name="grads",
    )(ids, in_hbm(prob), in_hbm(keys), in_hbm(gates), loss, *raws)


def kterm_kernel(ids, half_ref, gates_ref, q_t, other_ref, out_ref, coefs):
    step = pl.program_id(0)
    for tile in range(HALF // WIDE):

        @pl.when(step == tile)
        def _():
            coef_tile(coefs, half_ref[:, tile * WIDE : (tile + 1) * WIDE], gates_ref)
            kterm = kterm_tile(coefs, q_t)
            for i in range(WIDE // ROWS):
                place = ids[SORTED[tile * (WIDE // ROWS) + i]] >> 1
                place = pl.ds(pl.multiple_of(place * ROWS, ROWS), ROWS)
                part = kterm[i * ROWS : (i + 1) * ROWS, :] + other_ref[place, :]
                out_ref[place, :] = part.astype(jnp.bfloat16)


def kterm_call(ids, half, gates, q_t, other):
    out = jax.ShapeDtypeStruct((HALF, IDIM), jnp.bfloat16)
    return pl.pallas_call(
        kterm_kernel,
        out_shape=out,
        grid_spec=pltpu.PrefetchScalarGridSpec(
            num_scalar_prefetch=1,
            grid=(HALF // WIDE,),
            in_specs=[whole(half), GATES, whole(q_t), whole(other)],
            out_specs=whole(out),
            scratch_shapes=[pltpu.VMEM((PEERS * ROWS, WIDE), jnp.bfloat16)],
        ),
        compiler_params=pltpu.CompilerParams(vmem_limit_bytes=50 * MIB),
        cost_estimate=pl.CostEstimate(
            flops=2 * PEERS * ROWS * TOTAL * IDIM, bytes_accessed=12 * MIB, transcendentals=0
        ),
        name="kterms",
    )(ids, in_hbm(half), in_hbm(gates), in_hbm(q_t), other)


def shift(array, axis, size, by):
    return lax.ppermute(array, axis, [(i, (i + by) % size) for i in range(size)])


def local(
    main_queries, latents, saved_lse, index_queries, index_keys, head_weights, row_weight,
    block_offsets,
):
    c0, c1, c2 = (lax.axis_index(a) for a in CTX)
    head = lax.axis_index(HEAD)
    ids = [(c0 ^ a) * 8 + ((c1 + b) & 3) * 2 + (c2 ^ c) for a, b, c in ORDER]
    ids = jnp.stack([i.astype(jnp.int32) for i in ids + [head]])

    own = jnp.concatenate([index_keys, latents], axis=1)
    core = functools.partial(shift, axis="ctx_2", size=2, by=1)
    up = functools.partial(shift, axis="ctx_1", size=4, by=1)
    down = functools.partial(shift, axis="ctx_1", size=4, by=-1)
    side = functools.partial(shift, axis="ctx_0", size=2, by=1)

    weights = head_weights.reshape(PEERS, 2, IDIM)
    weights = jnp.pad(weights, ((0, 0), (0, PAD - 2), (0, 0)))
    qw = jnp.concatenate([index_queries.reshape(PEERS, ROWS, IDIM), weights], axis=1)

    q_t = jnp.transpose(main_queries, (1, 2, 0))
    lse_t = saved_lse.T
    loss = row_weight.reshape(ROWS // IDIM, IDIM)
    q_t, lse_t, loss, qw, ids = lax.optimization_barrier((q_t, lse_t, loss, qw, ids))
    mass = functools.partial(mass_call, ids, block_offsets, q_t, lse_t)

    q_t = jnp.transpose(main_queries, (1, 2, 0))
    lse_t = saved_lse.T
    loss = row_weight.reshape(ROWS // IDIM, IDIM)
    q_t, lse_t, loss, qw, ids = lax.optimization_barrier((q_t, lse_t, loss, qw, ids))
    mass = functools.partial(mass_call, ids, block_offsets, q_t, lse_t)

    pair = core(own)
    z, yp, ym = side(own), up(own), down(own)
    near, keys_0 = mass([own, pair], 0)
    z, yp, ym, near = lax.optimization_barrier((z, yp, ym, near))
    zyp, zym, y2 = up(z), down(z), up(yp)
    pz, pyp, pym = core(z), core(yp), core(ym)
    raw_0, keys_1 = mass([z, yp, ym, pz, pyp], 2, (qw, near))
    raw_0, pym = lax.optimization_barrier((raw_0, pym))
    held, keys_2 = mass([pym], 7)
    zyp, zym, held = lax.optimization_barrier((zyp, zym, held))
    pzyp, pzym, py2 = core(zyp), core(zym), core(y2)
    zy2, pzy2 = down(zym), up(pzyp)
    raw_0 = lax.all_to_all(raw_0, HEAD, 0, 0, tiled=True)
    far, keys_3 = mass([zyp, zym, y2, pzyp, pzym, py2], 8, (held,))
    raw_1, keys_4 = mass([zy2, pzy2], 14, (far,))
    raw_1 = lax.all_to_all(raw_1, HEAD, 0, 0, tiled=True)

    prob, keys, gates = prob_call(ids, block_offsets, loss, raw_0, (keys_0, keys_1, keys_2, keys_3, keys_4))
    qgrad, other, half, i_t = grad_call(
        ids, prob, keys, gates, loss, (raw_0, raw_1), (ROWS + PAD, 0)
    )
    other = core(other)
    qgrad = lax.all_to_all(qgrad, HEAD, 0, 0, tiled=True)
    kterm = kterm_call(ids, half, gates, i_t, other)
    kterm = kterm.reshape(HALF // SHARE, SHARE, IDIM)
    kterm = lax.all_to_all(kterm, CTX[:2] + HEAD, 0, 0, tiled=True)
    query_grads = qgrad.reshape(ROWS, PEERS, IDIM).astype(jnp.float32)
    key_grads = jnp.sum(kterm.astype(jnp.float32), axis=0)
    return query_grads, key_grads


def solution(mesh):
    torus = Mesh(mesh.devices.reshape(2, 4, 2, 4, 2), ALL)
    placed = (
        P(CTX, HEAD, None), P(CTX, None), P(CTX, HEAD), P(CTX, HEAD, None), P(CTX, None),
        P(CTX, HEAD), P(CTX), P(),
    )
    return jax.shard_map(
        local,
        mesh=torus,
        in_specs=placed,
        out_specs=(P(CTX, HEAD, None), P(ALL, None)),
        check_vma=False,
    )
```
